512 devices in a mesh: span: 16 (over y, x), leaf: 32 (over z, core).
Axes of the slice: x: 4, y: 4, z: 16, core: 2. Of those that a mesh axis runs over, the one named last changes fastest.
Arguments:
- populations: float32 [27, 256, 256, 128], P(None, 'span', 'leaf'), may hold values from 0.5 to 1.5
- relax_rates: float32 [27], replicated, may hold values from 1 to 1.6
- marker_forces: float32 [2, 3, 196608], P(None, None, ('span', 'leaf')), may hold values from -6 to 6
- marker_dest: int32 [2, 196608, 1], P(None, ('span', 'leaf')), may hold values from 0 to 31; in each aligned block of 384 rows (0 to 383, 384 to 767, ..., all dimensions but the last counted through in order) at most 36 rows name the same one
- marker_cells: int32 [2, 196608], P(None, ('span', 'leaf')), may hold values from 0 to 16383
Outputs:
- final_state: float32 [27, 256, 256, 128], P(None, 'span', 'leaf')
The draws below stay inside these ranges and needn't reach their ends.
Inputs may be any that keep to these rules, and one draw needn't show every extreme that they name: `marker_dest`: in each step, no destination is named by more than 36 of the 384 markers of one device, and in every draw some device's markers name one destination exactly 36 times.
All inputs are finite; a program needn't handle non-finite values.
Results may differ from the reference program's by a relative error of at most 0.0001.
Values sent between devices are 32-bit elements; how exact they have to be, the bound alone decides.
No kernel may reach another device: no remote copies, remote signals or barrier semaphores. Data moves between devices by JAX's collectives and lax.ppermute only.
A program may use at most 64 MiB of HBM per device.

```python
import math
import jax
import jax.numpy as jnp
import numpy as np
from jax import lax

CX = 16
CZ = 8
NY = 128
MARK_DEV = 384
STEPS = 2
CAP = 36
CELLS = 16384
NX = 256
NZ = 256
GROUP_MARKERS = 12288
MARKERS = 196608
N_LEAF = 32


def set_ends(result, own_key, smallest, top_value):
    index_at = [jax.random.randint(jax.random.fold_in(own_key, axis), (), 0, length) for axis, length in enumerate(result.shape)]
    longest = result.shape.index(max(result.shape))
    next_to = index_at[:longest] + [(index_at[longest] + 1) % result.shape[longest]] + index_at[longest + 1:]
    return result.at[tuple(index_at)].set(smallest).at[tuple(next_to)].set(top_value)


def levels(own_key, dims, split, least, top_value):
    loudness, own = 1.0, jax.random.fold_in(own_key, 6)
    for axis_at, shards_of in split:
        heights = jnp.exp(jax.random.uniform(jax.random.fold_in(own, axis_at), (shards_of,), jnp.float32, least / len(split), top_value / len(split)))
        loudness = loudness * jnp.repeat(heights, dims[axis_at] // shards_of).reshape([-1 if axis == axis_at else 1 for axis in range(len(dims))])
    return loudness


def deal_out(key, own, number, rows, number_of, top, reach, lean):
    order = jax.random.permutation(key, number_of)
    packed, common = portions_of(number_of, rows * top, reach, lean, True), portions_of(number_of, rows * top, reach, lean, False)
    places = jnp.arange(number_of)

    def named(lengths, turn):
        used = int((lengths > 0).sum())
        fixed = max(1, used // 4)
        shifted = fixed + (places - fixed + turn * (used - fixed)) % max(1, number_of - fixed)
        return jnp.zeros((number_of,), jnp.int32).at[order[jnp.where(places < fixed, places, shifted)]].set(jnp.asarray(lengths, jnp.int32))

    lengths = jnp.where(number % 4 == 0, named(packed, number // 4), named(common, number - number // 4 - 1))
    mixed = jax.random.permutation(jax.random.fold_in(own, 3), number_of)
    giver, receiver = mixed[0:number_of // 2 * 2:2], mixed[1:number_of // 2 * 2:2]
    margin = jnp.minimum(lengths[giver] - 1, reach - lengths[receiver]) // 2
    margin = jnp.where((giver == order[0]) | (receiver == order[0]) | (lengths[receiver] == 0), 0, jnp.maximum(margin, 0))
    shifted = jax.random.randint(jax.random.fold_in(own, 4), (number_of // 2,), 0, 1 << 20) % (margin + 1)
    lengths = lengths.at[giver].add(-shifted).at[receiver].add(shifted)
    items = jnp.searchsorted(jnp.cumsum(lengths), jnp.arange(rows * top), side="right").astype(jnp.int32)
    listing = items.reshape(top, rows).T
    listing = listing[jax.random.permutation(jax.random.fold_in(own, 1), rows)]
    turn = jax.random.randint(jax.random.fold_in(own, 2), (rows, 1), 0, top)
    return jnp.take_along_axis(listing, (jnp.arange(top)[None, :] + turn) % top, axis=1)


def portions_of(amount, total, reach, skew, full):
    portions = [(1 << 20) // math.isqrt(standing ** skew) + 1 for standing in range(1, amount + 1)]
    largest = reach if full else min(reach, max(-(-total // amount), total * portions[0] // sum(portions)))
    least = 1 if total - largest >= amount - 1 else 0
    given, spare = [largest] + [least] * (amount - 1), total - largest - least * (amount - 1)
    while spare > 0:
        movable = [i for i in range(1, amount) if given[i] < largest] or [i for i in range(1, amount) if given[i] < reach]
        whole, remaining = sum([portions[i] for i in movable]), spare
        for i in movable:
            addition = min(reach - given[i], max(1, remaining * portions[i] // whole), spare)
            given[i] = given[i] + addition
            spare = spare - addition
    return np.array(given)


def centred(rng, dims, spread, limit, split=(), kind=jnp.bfloat16):
    loudness = levels(rng, dims, split, -0.22, 0.18) if split else 1.0
    drawn = jax.random.normal(rng, dims, jnp.float32) * spread * loudness
    return jnp.minimum(jnp.maximum(drawn, -limit), limit).astype(kind)


def setup_inputs(seed: int = 0) -> dict:
    streams_of = jax.random.split(jax.random.key(seed), 6)
    populations = jnp.clip(0.5 + 1.0 * jax.random.uniform(streams_of[0], (27, NX, NZ, NY), jnp.float32) ** levels(streams_of[0], (27, NX, NZ, NY), ((1, 16), (2, 32)), -0.2, 0.2), 0.5, 1.5)
    relax_rates = jnp.clip(jnp.exp(jax.random.uniform(streams_of[1], (27,), jnp.float32, math.log(1.0), math.log(1.6))), 1.0, 1.6)
    marker_forces = centred(streams_of[2], (STEPS, 3, MARKERS), 1.0, 6.0, ((2, 512),), jnp.float32)
    marker_dest_keys = jax.random.split(jax.random.fold_in(streams_of[3], 1), STEPS * MARKERS // MARK_DEV)
    marker_dest_turns = jax.random.permutation(jax.random.fold_in(streams_of[3], 3), STEPS * MARKERS // MARK_DEV)
    marker_dest = jax.vmap(lambda own, number: deal_out(jax.random.fold_in(streams_of[3], 2), own, number, MARK_DEV, N_LEAF, 1, CAP, 2))(marker_dest_keys, marker_dest_turns).reshape((STEPS, MARKERS, 1))
    marker_cells = set_ends(jax.random.randint(streams_of[4], (STEPS, MARKERS), 0, CELLS), jax.random.fold_in(streams_of[4], 1), 0, CELLS - 1).astype(jnp.int32)
    return dict(populations=populations, relax_rates=relax_rates, marker_forces=marker_forces, marker_dest=marker_dest, marker_cells=marker_cells)


RHO_BASE = 27.0


def lattice_tables():
    axis_values = np.array([-1.0, 0.0, 1.0])
    powers = np.array([[1.0, 1.0, 1.0], [-1.0, 0.0, 1.0], [1.0, 0.0, 1.0]])
    inverse = np.array([[0.0, -0.5, 0.5], [1.0, 0.0, -1.0], [0.0, 0.5, 0.5]])
    forward = np.kron(np.kron(powers, powers), powers)
    backward = np.kron(np.kron(inverse, inverse), inverse)
    one_weight = np.array([1.0 / 6.0, 2.0 / 3.0, 1.0 / 6.0])
    weights = np.kron(np.kron(one_weight, one_weight), one_weight)
    velocity = np.stack(np.meshgrid(axis_values, axis_values, axis_values, indexing="ij"), 0).reshape(3, 27)
    return forward, backward, weights, velocity


def collide(populations, rates_cell, force_field, tables):
    forward = jnp.asarray(tables[0], dtype=jnp.float32)
    backward = jnp.asarray(tables[1], dtype=jnp.float32)
    weights = jnp.asarray(tables[2], dtype=jnp.float32)
    velocity = jnp.asarray(tables[3], dtype=jnp.float32)
    highest = lax.Precision.HIGHEST
    density = jnp.sum(populations, axis=0)
    momentum = jnp.einsum("dq,q...->d...", velocity, populations, precision=highest)
    velocity_field = momentum / RHO_BASE
    along = jnp.einsum("dq,d...->q...", velocity, velocity_field, precision=highest)
    square = jnp.sum(velocity_field * velocity_field, axis=0)
    shaped = weights.reshape((27,) + (1,) * (populations.ndim - 1))
    equilibrium = shaped * (density + RHO_BASE * (3.0 * along + 4.5 * along * along - 1.5 * square))
    moments = jnp.einsum("kq,q...->k...", forward, populations - equilibrium, precision=highest)
    relaxed = jnp.einsum("qk,k...->q...", backward, rates_cell * moments, precision=highest)
    source = 3.0 * shaped * jnp.einsum("dq,d...->q...", velocity, force_field, precision=highest)
    return populations - relaxed + source


def stream_whole(post, velocity):
    moved = []
    for direction in range(27):
        shift_x = int(velocity[0, direction])
        shift_y = int(velocity[1, direction])
        shift_z = int(velocity[2, direction])
        moved.append(jnp.roll(post[direction], (shift_x, shift_z, shift_y), axis=(0, 1, 2)))
    return jnp.stack(moved)


def reference(populations, relax_rates, marker_forces, marker_dest, marker_cells):
    tables = lattice_tables()
    rates_cell = relax_rates[:, None, None, None]
    marker_ids = jnp.arange(MARKERS, dtype=jnp.int32)
    span_ids = marker_ids // GROUP_MARKERS
    state = populations
    for time_step in range(STEPS):
        cell_ids = marker_cells[time_step]
        row_x = span_ids * CX + cell_ids // (CZ * NY)
        row_z = marker_dest[time_step, :, 0] * CZ + (cell_ids // NY) % CZ
        row_y = cell_ids % NY
        force_field = jnp.zeros((3, NX, NZ, NY), jnp.float32).at[:, row_x, row_z, row_y].add(marker_forces[time_step])
        post = collide(state, rates_cell, force_field, tables)
        state = stream_whole(post, tables[3])
    return state
```

```python
import functools
import jax
import jax.numpy as jnp
import numpy as np
from jax import lax
from jax.experimental import pallas as pl
from jax.experimental.pallas import tpu as pltpu
from jax.sharding import PartitionSpec as P

F32 = jnp.float32
BF16 = jnp.bfloat16
PLANES = 20
WHOLE = pl.BlockSpec(memory_space=pltpu.VMEM)
SCALARS = pl.BlockSpec(memory_space=pltpu.SMEM)
HBM = pl.BlockSpec(memory_space=pl.ANY)


def params(mib):
    return pltpu.CompilerParams(vmem_limit_bytes=mib * 2**20)


def components(q):
    return q // 9 - 1, (q // 3) % 3 - 1, q % 3 - 1


def transform(values, step):
    values = list(values)
    for stride in (9, 3, 1):
        for q in range(27):
            if (q // stride) % 3 == 0:
                triple = (q, q + stride, q + 2 * stride)
                for place, value in zip(triple, step(*[values[i] for i in triple])):
                    values[place] = value
    return values


def to_moments(low, middle, high):
    both = low + high
    return both + middle, high - low, both


def from_moments(zeroth, first, second):
    return second - first, zeroth - second, second + first


def collide(populations, rate, force):
    moments = transform(populations, to_moments)
    density = moments[0]
    momentum = (moments[9], moments[3], moments[1])
    velocity = [part * (1.0 / 27.0) for part in momentum]
    flux = [27.0 * part for part in velocity]
    energy = [3.0 * f * v for f, v in zip(flux, velocity)]
    cross = {}
    for i in range(3):
        for j in range(i + 1, 3):
            cross[i, j] = flux[i] * velocity[j]
    relaxed = []
    for k in range(27):
        powers = (k // 9, (k // 3) % 3, k % 3)
        odd = [i for i in range(3) if powers[i] == 1]
        squares = [i for i in range(3) if powers[i] == 2]
        share = 3.0 ** -len(squares)
        if len(odd) == 0:
            level = density
            for i in squares:
                level = level + energy[i]
        elif len(odd) == 1:
            level = flux[odd[0]]
        elif len(odd) == 2:
            level = cross[odd[0], odd[1]]
        else:
            level = None
        if level is not None and squares:
            level = level * share
        gap = moments[k] if level is None else moments[k] - level
        value = moments[k] - rate(k) * gap
        if force is not None and len(odd) == 1:
            push = force[odd[0]]
            value = value + (push * share if squares else push)
        relaxed.append(value)
    result = transform(relaxed, from_moments)
    scaled = []
    for q in range(27):
        moving = sum(1 for c in components(q) if c != 0)
        scaled.append(result[q] * 0.5**moving if moving else result[q])
    return scaled


def sources(force):
    weight = {1: 2.0 / 9.0, 2: 1.0 / 18.0, 3: 1.0 / 72.0}
    scaled = {n: [part * weight[n] for part in force] for n in weight}
    terms = [None] * 27
    for q in range(14, 27):
        c = components(q)
        total = None
        for i in range(3):
            if c[i] == 0:
                continue
            part = scaled[sum(1 for v in c if v != 0)][i]
            if total is None:
                total = part
            elif c[i] > 0:
                total = total + part
            else:
                total = total - part
        terms[q] = (total, 1)
        terms[26 - q] = (total, -1)
    return terms


def pushed(value, term):
    if term is None:
        return value
    return value + term[0] if term[1] > 0 else value - term[0]


def bin_kernel(forces_ref, dest_ref, cells_ref, sent_ref):
    markers = cells_ref.shape[1]
    leaves = sent_ref.shape[0]
    highest = lax.Precision.HIGHEST
    earlier = (
        lax.broadcasted_iota(jnp.int32, (markers, markers), 0)
        < lax.broadcasted_iota(jnp.int32, (markers, markers), 1)
    ).astype(F32).astype(BF16)
    hot = []
    for t in range(2):
        row = dest_ref[t]
        leaf = lax.broadcasted_iota(jnp.int32, (leaves, markers), 0)
        hot.append((leaf == row).astype(F32))
    ahead = jnp.dot(
        jnp.concatenate(hot, axis=0).astype(BF16), earlier, preferred_element_type=F32
    )
    left, right = [], []
    for t in range(2):
        rank = jnp.sum(hot[t] * ahead[t * leaves : (t + 1) * leaves], axis=0, keepdims=True)
        rank = rank.astype(jnp.int32)
        third = rank // 16
        left.append(jnp.concatenate([jnp.where(third == r, hot[t], 0.0) for r in range(3)], axis=0))
        spot = lax.broadcasted_iota(jnp.int32, (16, markers), 0) == rank % 16
        rows = [cells_ref[t : t + 1, :].astype(F32)] + [forces_ref[c, t : t + 1, :] for c in range(3)]
        own = jnp.concatenate([jnp.where(spot, row, 0.0) for row in rows], axis=0)
        none = jnp.zeros_like(own)
        right.append(jnp.concatenate([own, none] if t == 0 else [none, own], axis=0))
    packed = lax.dot_general(
        jnp.concatenate(left, axis=1),
        jnp.concatenate(right, axis=1),
        (((1,), (1,)), ((), ())),
        precision=highest,
        preferred_element_type=F32,
    )
    for r in range(3):
        sent_ref[:, r, :] = packed[r * leaves : (r + 1) * leaves]


def first_kernel(rates_ref, after_ref, populations_ref, collided_ref):
    width = populations_ref.shape[1]
    base = pl.program_id(0) * width

    def plane(x, carry):
        result = collide(
            [populations_ref[q, x] for q in range(27)], lambda k: rates_ref[k], None
        )
        for q in range(27):
            collided_ref[q, base + x] = result[q]
        return carry

    lax.fori_loop(0, width, plane, 0)


def rows_by_value(received_ref):
    blocks = []
    for r in range(2):
        whole = received_ref[:, r, :]
        blocks += [whole[8 * b : 8 * b + 8] for b in range(4)]
    lane = lax.broadcasted_iota(jnp.int32, (8, 128), 1)
    for half in (4, 2, 1):
        low = (lane // (16 * half)) % 2 == 0
        for b in range(8):
            if b & half:
                continue
            first, second = blocks[b], blocks[b + half]
            blocks[b] = jnp.where(low, first, pltpu.roll(second, 16 * half, 1))
            blocks[b + half] = jnp.where(low, pltpu.roll(first, 128 - 16 * half, 1), second)
    last = received_ref[:, 2, :]
    tail = None
    for b in range(4):
        part = last[8 * b : 8 * b + 8]
        part = jnp.where(lane % 16 < 4, part, 0.0)
        if b:
            part = pltpu.roll(part, 4 * b, 1)
        tail = part if tail is None else tail + part
    sub = lax.broadcasted_iota(jnp.int32, (8, 128), 0)
    rows = []
    for v in range(8):
        spread = pltpu.roll(tail, 128 - 16 * v, 1) if v else tail
        spread = pltpu.roll(spread, 0, 1, stride=16, stride_axis=0)
        spread = jnp.where(lane // 16 == sub, spread, 0.0)
        rows.append((blocks[v], jnp.sum(spread, axis=0, keepdims=True)))
    return rows


def deposit_kernel(parity_ref, received_ref, collided_ref, field_ref, a_ref, b_ref):
    rows = rows_by_value(received_ref)
    index = lax.broadcasted_iota(jnp.int32, (128, 128), 0)
    for t in range(2):
        values = rows[4 * t : 4 * t + 4]
        chunks = [[v[0][s : s + 1] for s in range(8)] + [v[1]] for v in values]
        outer, weighted = [], []
        for s in range(9):
            cell = chunks[0][s].astype(jnp.int32)
            outer.append((index == cell // 128).astype(F32).astype(BF16))
            inner = (index == cell % 128).astype(F32).astype(BF16)
            parts = []
            for c in range(3):
                amount = chunks[c + 1][s]
                big = amount.astype(BF16)
                small = (amount - big.astype(F32)).astype(BF16)
                parts.append((inner * big, inner * small))
            weighted.append(
                jnp.concatenate([p[0] for p in parts] + [p[1] for p in parts], axis=0)
            )
        field = lax.dot_general(
            jnp.concatenate(outer, axis=1),
            jnp.concatenate(weighted, axis=1),
            (((1,), (1,)), ((), ())),
            preferred_element_type=F32,
        )
        for c in range(3):
            whole = field[:, 128 * c : 128 * c + 128] + field[:, 384 + 128 * c : 512 + 128 * c]
            field_ref[t, c] = whole.reshape(field_ref.shape[2:])
    last = collided_ref.shape[1] - 1

    def layers(ref, sign, edge, inside):
        terms = sources([field_ref[0, c, edge] for c in range(3)])
        for n in range(18):
            q = 9 + n if n < 9 else 9 + 9 * sign + n - 9
            ref[n] = pushed(collided_ref[q, edge], terms[q])
        terms = sources([field_ref[0, c, inside] for c in range(3)])
        for n in range(9):
            q = 9 + 9 * sign + n
            ref[18 + n] = pushed(collided_ref[q, inside], terms[q])
        for c in range(3):
            ref[27 + c] = field_ref[1, c, edge]

    @pl.when(parity_ref[0] == 0)
    def _():
        layers(a_ref, 1, last, last - 1)
        layers(b_ref, -1, 0, 1)

    @pl.when(parity_ref[0] != 0)
    def _():
        layers(b_ref, 1, last, last - 1)
        layers(a_ref, -1, 0, 1)


def pack_kernel(parity_ref, collided_ref, field_ref, a_ref, b_ref, halo_ref, up_ref, down_ref):
    @pl.when(parity_ref[0] == 0)
    def _():
        halo_ref[0] = b_ref[...]
        halo_ref[1] = a_ref[...]

    @pl.when(parity_ref[0] != 0)
    def _():
        halo_ref[0] = a_ref[...]
        halo_ref[1] = b_ref[...]

    width = collided_ref.shape[1]
    top = collided_ref.shape[2] - 1
    for ref, sign, edge, inside in ((up_ref, 1, top, top - 1), (down_ref, -1, 0, 1)):
        for ring, z, kinds in ((0, edge, (0, sign)), (1, inside, (sign,))):
            terms = sources([field_ref[0, c, :, z, :] for c in range(3)])
            for order, cz in enumerate(kinds):
                for j in range(9):
                    q = 3 * j + cz + 1
                    place = 18 * ring + 9 * order + j
                    ref[place, pl.ds(2, width), :] = pushed(collided_ref[q, :, z, :], terms[q])
                    cx = j // 3 - 1
                    n = 3 * (j % 3) + cz + 1
                    for side, toward, near, far in ((0, 1, 1, 0), (1, -1, width + 2, width + 3)):
                        if cx == 0:
                            ref[place, pl.ds(near, 1), :] = halo_ref[side, n, pl.ds(z, 1), :]
                        if cx == toward:
                            ref[place, pl.ds(near, 1), :] = halo_ref[side, 9 + n, pl.ds(z, 1), :]
                            ref[place, pl.ds(far, 1), :] = halo_ref[side, 18 + n, pl.ds(z, 1), :]
        for c in range(3):
            ref[27 + c, pl.ds(2, width), :] = field_ref[1, c, :, edge, :]
            ref[27 + c, pl.ds(1, 1), :] = halo_ref[0, 27 + c, pl.ds(edge, 1), :]
            ref[27 + c, pl.ds(width + 2, 1), :] = halo_ref[1, 27 + c, pl.ds(edge, 1), :]


def final_kernel(
    rates_ref, collided_ref, field_ref, halo_ref, up_ref, down_ref, low_ref, high_ref,
    out_ref, state, ring, result, sems,
):
    width, height = collided_ref.shape[1:3]
    sub = lax.broadcasted_iota(jnp.int32, (height, 128), 0)

    def moved(tile, q, low_row, high_row):
        _, cy, cz = components(q)
        if cz > 0:
            tile = jnp.where(sub == 0, low_row(), pltpu.roll(tile, 1, 0))
        elif cz < 0:
            tile = jnp.where(sub == height - 1, high_row(), pltpu.roll(tile, height - 1, 0))
        return pltpu.roll(tile, cy % 128, 1) if cy else tile

    def first_rows(q, row):
        place = 9 + q // 3
        return (
            lambda: low_ref[place, pl.ds(row, 1), :],
            lambda: high_ref[place, pl.ds(row, 1), :],
        )

    def own(x, carry):
        terms = sources([field_ref[0, c, x] for c in range(3)])
        for q in range(27):
            tile = pushed(collided_ref[q, x], terms[q])
            state[q, x + 2 + q // 9 - 1] = moved(tile, q, *first_rows(q, x + 2))
        return carry

    lax.fori_loop(0, width, own, 0)
    for side, toward, near in ((0, 1, 1), (1, -1, width + 2)):
        for n in range(18):
            q = 9 + n if n < 9 else 9 + 9 * toward + n - 9
            tile = halo_ref[side, n]
            state[q, near + q // 9 - 1] = moved(tile, q, *first_rows(q, near))
        for n in range(9):
            q = 9 + 9 * toward + n
            tile = halo_ref[side, 18 + n]
            state[q, near] = moved(tile, q, *first_rows(q, near - toward))

    rate = lambda k: rates_ref[k]
    for side, got, own_sent, toward in ((0, low_ref, down_ref, 1), (1, high_ref, up_ref, -1)):

        def edge(block, carry, side=side, got=got, own_sent=own_sent, toward=toward):
            start = jnp.where(block == 2, 11, 1 + 8 * block)
            values = []
            for q in range(27):
                cx, cy, cz = components(q)
                j = q // 3
                where = pl.ds(start - cx, 8)
                if cz == toward:
                    row = got[18 + j, where, :]
                elif cz == 0:
                    row = got[j, where, :]
                else:
                    row = own_sent[9 + j, where, :]
                values.append(pltpu.roll(row, cy % 128, 1) if cy else row)
            force = [got[27 + c, pl.ds(start, 8), :] for c in range(3)]
            after = collide(values, rate, force)
            for j in range(9):
                ring[side, j, pl.ds(start, 8), :] = after[3 * j + toward + 1]
            return carry

        lax.fori_loop(0, 3, edge, 0)

    def second(x, force):
        after = collide([state[q, x] for q in range(27)], rate, force)
        for q in range(27):
            j = q // 3
            result[q, x + q // 9 - 1] = moved(
                after[q],
                q,
                lambda: ring[0, j, pl.ds(x, 1), :],
                lambda: ring[1, j, pl.ds(x, 1), :],
            )

    second(1, [halo_ref[0, 27 + c] for c in range(3)])
    chunk = 4
    parts = width // chunk

    def copy(part):
        return pltpu.make_async_copy(
            result.at[:, pl.ds(2 + part * chunk, chunk)],
            out_ref.at[:, pl.ds(part * chunk, chunk)],
            sems.at[part],
        )

    def inner(x, carry):
        second(x + 2, [field_ref[1, c, x] for c in range(3)])
        return carry

    done = 0
    for part in range(parts):
        until = min(width, (part + 1) * chunk + 1)
        lax.fori_loop(done, until, inner, 0)
        done = until
        if part == parts - 1:
            second(width + 2, [halo_ref[1, 27 + c] for c in range(3)])
        copy(part).start()
    for part in range(parts):
        copy(part).wait()


def cost(flops, moved):
    return pl.CostEstimate(flops=flops, bytes_accessed=moved, transcendentals=0)


def body(populations, relax_rates, marker_forces, marker_dest, marker_cells):
    width, height, length = populations.shape[1:]
    leaves = lax.axis_size("leaf")
    spans = lax.axis_size("span")
    markers = marker_cells.shape[1]
    held = functools.partial(pltpu.with_memory_space_constraint, memory_space=pltpu.VMEM)
    near = lambda *shape: pltpu.VMEM(shape, F32)
    sent = pl.pallas_call(
        bin_kernel,
        out_shape=near(leaves, 3, 128),
        in_specs=[WHOLE] * 3,
        out_specs=WHOLE,
        compiler_params=params(16),
        name="bin_markers",
    )(
        jnp.transpose(marker_forces, (1, 0, 2)),
        jnp.transpose(marker_dest, (0, 2, 1)),
        marker_cells,
    )
    received = lax.all_to_all(sent, "leaf", 0, 0, tiled=True)
    block = 2
    collided = pl.pallas_call(
        first_kernel,
        grid=(width // block,),
        out_shape=near(*populations.shape),
        in_specs=[
            SCALARS,
            HBM,
            pl.BlockSpec((27, block, height, length), lambda i: (0, i, 0, 0)),
        ],
        out_specs=WHOLE,
        compiler_params=params(16),
        cost_estimate=cost(27 * 12 * width * height * length, 8 * populations.size),
        name="collide_first",
    )(relax_rates, sent, populations)
    parity = lax.rem(lax.axis_index("span"), 2).astype(jnp.int32).reshape(1)
    layer = near(30, height, length)
    field, a_sent, b_sent = pl.pallas_call(
        deposit_kernel,
        out_shape=[near(2, 3, width, height, length), layer, layer],
        in_specs=[SCALARS, WHOLE, WHOLE],
        out_specs=[WHOLE] * 3,
        compiler_params=params(24),
        name="deposit",
    )(parity, held(received), held(collided))
    a_pairs = [(s, s ^ 1) for s in range(spans)]
    b_pairs = [(s, (s + 1 if s % 2 else s - 1) % spans) for s in range(spans)]
    a_got = lax.ppermute(a_sent, "span", a_pairs)
    b_got = lax.ppermute(b_sent, "span", b_pairs)
    face = near(30, 24, length)
    halo, up, down = pl.pallas_call(
        pack_kernel,
        out_shape=[near(2, 30, height, length), face, face],
        in_specs=[SCALARS] + [WHOLE] * 4,
        out_specs=[WHOLE] * 3,
        compiler_params=params(16),
        name="pack_layers",
    )(parity, held(collided), held(field), held(a_got), held(b_got))
    low = lax.ppermute(up, "leaf", [(l, (l + 1) % leaves) for l in range(leaves)])
    high = lax.ppermute(down, "leaf", [(l, (l - 1) % leaves) for l in range(leaves)])
    return pl.pallas_call(
        final_kernel,
        out_shape=jax.ShapeDtypeStruct(populations.shape, F32),
        in_specs=[SCALARS] + [WHOLE] * 7,
        out_specs=HBM,
        scratch_shapes=[
            pltpu.VMEM((27, PLANES, height, length), F32),
            pltpu.VMEM((2, 9, 24, length), F32),
            pltpu.VMEM((27, PLANES, height, length), F32),
            pltpu.SemaphoreType.DMA((width // 4,)),
        ],
        compiler_params=params(32),
        name="collide_second",
    )(relax_rates, held(collided), held(field), held(halo), held(up), held(down), held(low), held(high))


def solution(mesh):
    placed = (
        P(None, "span", "leaf", None),
        P(),
        P(None, None, ("span", "leaf")),
        P(None, ("span", "leaf"), None),
        P(None, ("span", "leaf")),
    )
    return jax.shard_map(
        body, mesh=mesh, in_specs=placed, out_specs=P(None, "span", "leaf", None), check_vma=False
    )
```

```python
import functools
import jax
import jax.numpy as jnp
import numpy as np
from jax import lax
from jax.experimental import pallas as pl
from jax.experimental.pallas import tpu as pltpu
from jax.sharding import PartitionSpec as P

F32 = jnp.float32
BF16 = jnp.bfloat16
PLANES = 20
WHOLE = pl.BlockSpec(memory_space=pltpu.VMEM)
SCALARS = pl.BlockSpec(memory_space=pltpu.SMEM)
HBM = pl.BlockSpec(memory_space=pl.ANY)


def params(mib):
    return pltpu.CompilerParams(vmem_limit_bytes=mib * 2**20)


def components(q):
    return q // 9 - 1, (q // 3) % 3 - 1, q % 3 - 1


def transform(values, step):
    values = list(values)
    for stride in (9, 3, 1):
        for q in range(27):
            if (q // stride) % 3 == 0:
                triple = (q, q + stride, q + 2 * stride)
                for place, value in zip(triple, step(*[values[i] for i in triple])):
                    values[place] = value
    return values


def to_moments(low, middle, high):
    both = low + high
    return both + middle, high - low, both


def from_moments(zeroth, first, second):
    return second - first, zeroth - second, second + first


def collide(populations, rate, force):
    moments = transform(populations, to_moments)
    density = moments[0]
    momentum = (moments[9], moments[3], moments[1])
    velocity = [part * (1.0 / 27.0) for part in momentum]
    flux = [27.0 * part for part in velocity]
    energy = [3.0 * f * v for f, v in zip(flux, velocity)]
    cross = {}
    for i in range(3):
        for j in range(i + 1, 3):
            cross[i, j] = flux[i] * velocity[j]
    relaxed = []
    for k in range(27):
        powers = (k // 9, (k // 3) % 3, k % 3)
        odd = [i for i in range(3) if powers[i] == 1]
        squares = [i for i in range(3) if powers[i] == 2]
        share = 3.0 ** -len(squares)
        if len(odd) == 0:
            level = density
            for i in squares:
                level = level + energy[i]
        elif len(odd) == 1:
            level = flux[odd[0]]
        elif len(odd) == 2:
            level = cross[odd[0], odd[1]]
        else:
            level = None
        if level is not None and squares:
            level = level * share
        gap = moments[k] if level is None else moments[k] - level
        value = moments[k] - rate(k) * gap
        if force is not None and len(odd) == 1:
            push = force[odd[0]]
            value = value + (push * share if squares else push)
        relaxed.append(value)
    result = transform(relaxed, from_moments)
    scaled = []
    for q in range(27):
        moving = sum(1 for c in components(q) if c != 0)
        scaled.append(result[q] * 0.5**moving if moving else result[q])
    return scaled


def sources(force):
    weight = {1: 2.0 / 9.0, 2: 1.0 / 18.0, 3: 1.0 / 72.0}
    scaled = {n: [part * weight[n] for part in force] for n in weight}
    terms = [None] * 27
    for q in range(14, 27):
        c = components(q)
        total = None
        for i in range(3):
            if c[i] == 0:
                continue
            part = scaled[sum(1 for v in c if v != 0)][i]
            if total is None:
                total = part
            elif c[i] > 0:
                total = total + part
            else:
                total = total - part
        terms[q] = (total, 1)
        terms[26 - q] = (total, -1)
    return terms


def pushed(value, term):
    if term is None:
        return value
    return value + term[0] if term[1] > 0 else value - term[0]


def group_order(leaves):
    root = leaves // 2
    return [root] + [leaf for leaf in range(leaves) if leaf != root]


def bin_kernel(forces_hbm, dest_hbm, cells_hbm, sent_ref, forces_ref, dest_ref, cells_ref, sems):
    pairs = ((dest_hbm, dest_ref), (cells_hbm, cells_ref), (forces_hbm, forces_ref))
    copies = [pltpu.make_async_copy(a, b, sems.at[i]) for i, (a, b) in enumerate(pairs)]
    for each in copies:
        each.start()
    for each in copies:
        each.wait()
    markers = cells_ref.shape[1]
    leaves = sent_ref.shape[0]
    root = leaves // 2
    highest = lax.Precision.HIGHEST
    earlier = (
        lax.broadcasted_iota(jnp.int32, (markers, markers), 0)
        < lax.broadcasted_iota(jnp.int32, (markers, markers), 1)
    ).astype(F32).astype(BF16)
    hot = []
    for t in range(2):
        row = dest_ref[t]
        row = jnp.where(row < root, row + 1, jnp.where(row == root, 0, row))
        leaf = lax.broadcasted_iota(jnp.int32, (leaves, markers), 0)
        hot.append((leaf == row).astype(F32))
    ahead = jnp.dot(
        jnp.concatenate(hot, axis=0).astype(BF16), earlier, preferred_element_type=F32
    )
    left, right = [], []
    for t in range(2):
        rank = jnp.sum(hot[t] * ahead[t * leaves : (t + 1) * leaves], axis=0, keepdims=True)
        rank = rank.astype(jnp.int32)
        third = rank // 16
        left.append(jnp.concatenate([jnp.where(third == r, hot[t], 0.0) for r in range(3)], axis=0))
        spot = lax.broadcasted_iota(jnp.int32, (16, markers), 0) == rank % 16
        rows = [cells_ref[t : t + 1, :].astype(F32)] + [forces_ref[c, t : t + 1, :] for c in range(3)]
        own = jnp.concatenate([jnp.where(spot, row, 0.0) for row in rows], axis=0)
        none = jnp.zeros_like(own)
        right.append(jnp.concatenate([own, none] if t == 0 else [none, own], axis=0))
    packed = lax.dot_general(
        jnp.concatenate(left, axis=1),
        jnp.concatenate(right, axis=1),
        (((1,), (1,)), ((), ())),
        precision=highest,
        preferred_element_type=F32,
    )
    for r in range(3):
        sent_ref[:, r, :] = packed[r * leaves : (r + 1) * leaves]


def first_kernel(rates_ref, after_ref, populations_ref, collided_ref):
    width = populations_ref.shape[1]
    base = pl.program_id(0) * width

    def plane(x, carry):
        result = collide(
            [populations_ref[q, x] for q in range(27)], lambda k: rates_ref[k], None
        )
        for q in range(27):
            collided_ref[q, base + x] = result[q]
        return carry

    lax.fori_loop(0, width, plane, 0)


def rows_by_value(received_ref):
    blocks = []
    for r in range(2):
        whole = received_ref[:, r, :]
        blocks += [whole[8 * b : 8 * b + 8] for b in range(4)]
    lane = lax.broadcasted_iota(jnp.int32, (8, 128), 1)
    for half in (4, 2, 1):
        low = (lane // (16 * half)) % 2 == 0
        for b in range(8):
            if b & half:
                continue
            first, second = blocks[b], blocks[b + half]
            blocks[b] = jnp.where(low, first, pltpu.roll(second, 16 * half, 1))
            blocks[b + half] = jnp.where(low, pltpu.roll(first, 128 - 16 * half, 1), second)
    last = received_ref[:, 2, :]
    tail = None
    for b in range(4):
        part = last[8 * b : 8 * b + 8]
        part = jnp.where(lane % 16 < 4, part, 0.0)
        if b:
            part = pltpu.roll(part, 4 * b, 1)
        tail = part if tail is None else tail + part
    sub = lax.broadcasted_iota(jnp.int32, (8, 128), 0)
    rows = []
    for v in range(8):
        spread = pltpu.roll(tail, 128 - 16 * v, 1) if v else tail
        spread = pltpu.roll(spread, 0, 1, stride=16, stride_axis=0)
        spread = jnp.where(lane // 16 == sub, spread, 0.0)
        rows.append((blocks[v], jnp.sum(spread, axis=0, keepdims=True)))
    return rows


def deposit_kernel(parity_ref, received_ref, collided_ref, field_ref, a_ref, b_ref):
    rows = rows_by_value(received_ref)
    index = lax.broadcasted_iota(jnp.int32, (128, 128), 0)
    for t in range(2):
        values = rows[4 * t : 4 * t + 4]
        chunks = [[v[0][s : s + 1] for s in range(8)] + [v[1]] for v in values]
        outer, weighted = [], []
        for s in range(9):
            cell = chunks[0][s].astype(jnp.int32)
            outer.append((index == cell // 128).astype(F32).astype(BF16))
            inner = (index == cell % 128).astype(F32).astype(BF16)
            parts = []
            for c in range(3):
                amount = chunks[c + 1][s]
                big = amount.astype(BF16)
                small = (amount - big.astype(F32)).astype(BF16)
                parts.append((inner * big, inner * small))
            weighted.append(
                jnp.concatenate([p[0] for p in parts] + [p[1] for p in parts], axis=0)
            )
        field = lax.dot_general(
            jnp.concatenate(outer, axis=1),
            jnp.concatenate(weighted, axis=1),
            (((1,), (1,)), ((), ())),
            preferred_element_type=F32,
        )
        for c in range(3):
            whole = field[:, 128 * c : 128 * c + 128] + field[:, 384 + 128 * c : 512 + 128 * c]
            field_ref[t, c] = whole.reshape(field_ref.shape[2:])
    last = collided_ref.shape[1] - 1

    def layers(ref, sign, edge, inside):
        terms = sources([field_ref[0, c, edge] for c in range(3)])
        for n in range(18):
            q = 9 + n if n < 9 else 9 + 9 * sign + n - 9
            ref[n] = pushed(collided_ref[q, edge], terms[q])
        terms = sources([field_ref[0, c, inside] for c in range(3)])
        for n in range(9):
            q = 9 + 9 * sign + n
            ref[18 + n] = pushed(collided_ref[q, inside], terms[q])
        for c in range(3):
            ref[27 + c] = field_ref[1, c, edge]

    @pl.when(parity_ref[0] == 0)
    def _():
        layers(a_ref, 1, last, last - 1)
        layers(b_ref, -1, 0, 1)

    @pl.when(parity_ref[0] != 0)
    def _():
        layers(b_ref, 1, last, last - 1)
        layers(a_ref, -1, 0, 1)


def pack_kernel(parity_ref, collided_ref, field_ref, a_ref, b_ref, halo_ref, up_ref, down_ref):
    @pl.when(parity_ref[0] == 0)
    def _():
        halo_ref[0] = b_ref[...]
        halo_ref[1] = a_ref[...]

    @pl.when(parity_ref[0] != 0)
    def _():
        halo_ref[0] = a_ref[...]
        halo_ref[1] = b_ref[...]

    width = collided_ref.shape[1]
    top = collided_ref.shape[2] - 1
    for ref, sign, edge, inside in ((up_ref, 1, top, top - 1), (down_ref, -1, 0, 1)):
        for ring, z, kinds in ((0, edge, (0, sign)), (1, inside, (sign,))):
            terms = sources([field_ref[0, c, :, z, :] for c in range(3)])
            for order, cz in enumerate(kinds):
                for j in range(9):
                    q = 3 * j + cz + 1
                    place = 18 * ring + 9 * order + j
                    ref[place, pl.ds(2, width), :] = pushed(collided_ref[q, :, z, :], terms[q])
                    cx = j // 3 - 1
                    n = 3 * (j % 3) + cz + 1
                    for side, toward, near, far in ((0, 1, 1, 0), (1, -1, width + 2, width + 3)):
                        if cx == 0:
                            ref[place, pl.ds(near, 1), :] = halo_ref[side, n, pl.ds(z, 1), :]
                        if cx == toward:
                            ref[place, pl.ds(near, 1), :] = halo_ref[side, 9 + n, pl.ds(z, 1), :]
                            ref[place, pl.ds(far, 1), :] = halo_ref[side, 18 + n, pl.ds(z, 1), :]
        for c in range(3):
            ref[27 + c, pl.ds(2, width), :] = field_ref[1, c, :, edge, :]
            ref[27 + c, pl.ds(1, 1), :] = halo_ref[0, 27 + c, pl.ds(edge, 1), :]
            ref[27 + c, pl.ds(width + 2, 1), :] = halo_ref[1, 27 + c, pl.ds(edge, 1), :]


def stream_kernel(collided_ref, field_ref, state):
    width, height = collided_ref.shape[1:3]

    def own(x, carry):
        terms = sources([field_ref[0, c, x] for c in range(3)])
        for q in range(27):
            cx, cy, cz = components(q)
            tile = pushed(collided_ref[q, x], terms[q])
            if cz:
                tile = pltpu.roll(tile, cz % height, 0)
            if cy:
                tile = pltpu.roll(tile, cy % 128, 1)
            state[q, x + 2 + cx] = tile
        return carry

    lax.fori_loop(0, width, own, 0)


def final_kernel(
    rates_ref, state_in, field_ref, halo_ref, up_ref, down_ref, low_ref, high_ref,
    out_ref, state, ring, result, sems,
):
    width, height = field_ref.shape[2:4]
    sub = lax.broadcasted_iota(jnp.int32, (height, 128), 0)

    def moved(tile, q, low_row, high_row):
        _, cy, cz = components(q)
        if cz > 0:
            tile = jnp.where(sub == 0, low_row(), pltpu.roll(tile, 1, 0))
        elif cz < 0:
            tile = jnp.where(sub == height - 1, high_row(), pltpu.roll(tile, height - 1, 0))
        return pltpu.roll(tile, cy % 128, 1) if cy else tile

    def first_rows(q, row):
        place = 9 + q // 3
        return (
            lambda: low_ref[place, pl.ds(row, 1), :],
            lambda: high_ref[place, pl.ds(row, 1), :],
        )

    for q in range(27):
        cx, cy, cz = components(q)
        if cz == 0:
            continue
        got, z = (low_ref, 0) if cz > 0 else (high_ref, height - 1)
        rows = got[9 + q // 3, pl.ds(2, width), :]
        state[q, pl.ds(2 + cx, width), z, :] = pltpu.roll(rows, cy % 128, 1) if cy else rows
    for side, toward, near in ((0, 1, 1), (1, -1, width + 2)):
        for n in range(18):
            q = 9 + n if n < 9 else 9 + 9 * toward + n - 9
            tile = halo_ref[side, n]
            state[q, near + q // 9 - 1] = moved(tile, q, *first_rows(q, near))
        for n in range(9):
            q = 9 + 9 * toward + n
            tile = halo_ref[side, 18 + n]
            state[q, near] = moved(tile, q, *first_rows(q, near - toward))

    rate = lambda k: rates_ref[k]
    for side, got, own_sent, toward in ((0, low_ref, down_ref, 1), (1, high_ref, up_ref, -1)):

        def edge(block, carry, side=side, got=got, own_sent=own_sent, toward=toward):
            start = jnp.where(block == 2, 11, 1 + 8 * block)
            values = []
            for q in range(27):
                cx, cy, cz = components(q)
                j = q // 3
                where = pl.ds(start - cx, 8)
                if cz == toward:
                    row = got[18 + j, where, :]
                elif cz == 0:
                    row = got[j, where, :]
                else:
                    row = own_sent[9 + j, where, :]
                values.append(pltpu.roll(row, cy % 128, 1) if cy else row)
            force = [got[27 + c, pl.ds(start, 8), :] for c in range(3)]
            after = collide(values, rate, force)
            for j in range(9):
                ring[side, j, pl.ds(start, 8), :] = after[3 * j + toward + 1]
            return carry

        lax.fori_loop(0, 3, edge, 0)

    def second(x, force):
        after = collide([state[q, x] for q in range(27)], rate, force)
        for q in range(27):
            j = q // 3
            result[q, x + q // 9 - 1] = moved(
                after[q],
                q,
                lambda: ring[0, j, pl.ds(x, 1), :],
                lambda: ring[1, j, pl.ds(x, 1), :],
            )

    second(1, [halo_ref[0, 27 + c] for c in range(3)])
    chunk = 2
    parts = width // chunk

    def copy(part):
        return pltpu.make_async_copy(
            result.at[:, pl.ds(2 + part * chunk, chunk)],
            out_ref.at[:, pl.ds(part * chunk, chunk)],
            sems.at[part],
        )

    def inner(x, carry):
        second(x + 2, [field_ref[1, c, x] for c in range(3)])
        return carry

    done = 0
    for part in range(parts):
        until = min(width, (part + 1) * chunk + 1)
        lax.fori_loop(done, until, inner, 0)
        done = until
        if part == parts - 1:
            second(width + 2, [halo_ref[1, 27 + c] for c in range(3)])
        copy(part).start()
    for part in range(parts):
        copy(part).wait()


def cost(flops, moved):
    return pl.CostEstimate(flops=flops, bytes_accessed=moved, transcendentals=0)


def body(populations, relax_rates, marker_forces, marker_dest, marker_cells):
    width, height, length = populations.shape[1:]
    leaves = lax.axis_size("leaf")
    spans = lax.axis_size("span")
    markers = marker_cells.shape[1]
    held = functools.partial(pltpu.with_memory_space_constraint, memory_space=pltpu.VMEM)
    far = functools.partial(pltpu.with_memory_space_constraint, memory_space=pltpu.HBM)
    near = lambda *shape: pltpu.VMEM(shape, F32)
    sent = pl.pallas_call(
        bin_kernel,
        out_shape=near(leaves, 3, 128),
        in_specs=[HBM] * 3,
        out_specs=WHOLE,
        scratch_shapes=[
            pltpu.VMEM((3, 2, markers), F32),
            pltpu.VMEM((2, 1, markers), jnp.int32),
            pltpu.VMEM((2, markers), jnp.int32),
            pltpu.SemaphoreType.DMA((3,)),
        ],
        compiler_params=params(16),
        name="bin_markers",
    )(
        far(jnp.transpose(marker_forces, (1, 0, 2))),
        far(jnp.transpose(marker_dest, (0, 2, 1))),
        far(marker_cells),
    )
    received = lax.all_to_all(
        sent, "leaf", 0, 0, tiled=True, axis_index_groups=[group_order(leaves)]
    )
    block = 2
    collided = pl.pallas_call(
        first_kernel,
        grid=(width // block,),
        out_shape=near(*populations.shape),
        in_specs=[
            SCALARS,
            HBM,
            pl.BlockSpec((27, block, height, length), lambda i: (0, i, 0, 0)),
        ],
        out_specs=WHOLE,
        compiler_params=params(16),
        cost_estimate=cost(27 * 12 * width * height * length, 8 * populations.size),
        name="collide_first",
    )(relax_rates, sent, populations)
    parity = lax.rem(lax.axis_index("span"), 2).astype(jnp.int32).reshape(1)
    layer = near(30, height, length)
    field, a_sent, b_sent = pl.pallas_call(
        deposit_kernel,
        out_shape=[near(2, 3, width, height, length), layer, layer],
        in_specs=[SCALARS, WHOLE, WHOLE],
        out_specs=[WHOLE] * 3,
        compiler_params=params(24),
        name="deposit",
    )(parity, held(received), held(collided))
    a_pairs = [(s, s ^ 1) for s in range(spans)]
    b_pairs = [(s, (s + 1 if s % 2 else s - 1) % spans) for s in range(spans)]
    a_got = lax.ppermute(a_sent, "span", a_pairs)
    b_got = lax.ppermute(b_sent, "span", b_pairs)
    face = near(30, 24, length)
    state = near(27, PLANES, height, length)
    streamed = pl.pallas_call(
        stream_kernel,
        out_shape=state,
        in_specs=[WHOLE] * 2,
        out_specs=WHOLE,
        compiler_params=params(16),
        cost_estimate=cost(27 * 12 * width * height * length, 8 * populations.size),
        name="stream_first",
    )(held(collided), held(field))
    halo, up, down = pl.pallas_call(
        pack_kernel,
        out_shape=[near(2, 30, height, length), face, face],
        in_specs=[SCALARS] + [WHOLE] * 4,
        out_specs=[WHOLE] * 3,
        compiler_params=params(16),
        name="pack_layers",
    )(parity, held(collided), held(field), held(a_got), held(b_got))
    low = lax.ppermute(up, "leaf", [(l, (l + 1) % leaves) for l in range(leaves)])
    high = lax.ppermute(down, "leaf", [(l, (l - 1) % leaves) for l in range(leaves)])
    return pl.pallas_call(
        final_kernel,
        out_shape=[jax.ShapeDtypeStruct(populations.shape, F32), state],
        in_specs=[SCALARS] + [WHOLE] * 7,
        out_specs=[HBM, WHOLE],
        input_output_aliases={1: 1},
        scratch_shapes=[
            pltpu.VMEM((2, 9, 24, length), F32),
            pltpu.VMEM((27, PLANES, height, length), F32),
            pltpu.SemaphoreType.DMA((width // 2,)),
        ],
        compiler_params=params(24),
        name="collide_second",
    )(relax_rates, held(streamed), held(field), held(halo), held(up), held(down), held(low), held(high))[0]


def solution(mesh):
    placed = (
        P(None, "span", "leaf", None),
        P(),
        P(None, None, ("span", "leaf")),
        P(None, ("span", "leaf"), None),
        P(None, ("span", "leaf")),
    )
    return jax.shard_map(
        body, mesh=mesh, in_specs=placed, out_specs=P(None, "span", "leaf", None), check_vma=False
    )
```

```python
import functools
import jax
import jax.numpy as jnp
import numpy as np
from jax import lax
from jax.experimental import pallas as pl
from jax.experimental.pallas import tpu as pltpu
from jax.sharding import PartitionSpec as P

F32 = jnp.float32
BF16 = jnp.bfloat16
SPLIT = 7
PLANES = 20
WHOLE = pl.BlockSpec(memory_space=pltpu.VMEM)
SCALARS = pl.BlockSpec(memory_space=pltpu.SMEM)
HBM = pl.BlockSpec(memory_space=pl.ANY)


def params(mib):
    return pltpu.CompilerParams(vmem_limit_bytes=mib * 2**20)


def components(q):
    return q // 9 - 1, (q // 3) % 3 - 1, q % 3 - 1


def transform(values, step):
    values = list(values)
    for stride in (9, 3, 1):
        for q in range(27):
            if (q // stride) % 3 == 0:
                triple = (q, q + stride, q + 2 * stride)
                for place, value in zip(triple, step(*[values[i] for i in triple])):
                    values[place] = value
    return values


def to_moments(low, middle, high):
    both = low + high
    return both + middle, high - low, both


def from_moments(zeroth, first, second):
    return second - first, zeroth - second, second + first


def collide(populations, rate, force):
    moments = transform(populations, to_moments)
    density = moments[0]
    momentum = (moments[9], moments[3], moments[1])
    velocity = [part * (1.0 / 27.0) for part in momentum]
    flux = [27.0 * part for part in velocity]
    energy = [3.0 * f * v for f, v in zip(flux, velocity)]
    cross = {}
    for i in range(3):
        for j in range(i + 1, 3):
            cross[i, j] = flux[i] * velocity[j]
    relaxed = []
    for k in range(27):
        powers = (k // 9, (k // 3) % 3, k % 3)
        odd = [i for i in range(3) if powers[i] == 1]
        squares = [i for i in range(3) if powers[i] == 2]
        share = 3.0 ** -len(squares)
        if len(odd) == 0:
            level = density
            for i in squares:
                level = level + energy[i]
        elif len(odd) == 1:
            level = flux[odd[0]]
        elif len(odd) == 2:
            level = cross[odd[0], odd[1]]
        else:
            level = None
        if level is not None and squares:
            level = level * share
        gap = moments[k] if level is None else moments[k] - level
        value = moments[k] - rate(k) * gap
        if force is not None and len(odd) == 1:
            push = force[odd[0]]
            value = value + (push * share if squares else push)
        relaxed.append(value)
    result = transform(relaxed, from_moments)
    scaled = []
    for q in range(27):
        moving = sum(1 for c in components(q) if c != 0)
        scaled.append(result[q] * 0.5**moving if moving else result[q])
    return scaled


def sources(force):
    weight = {1: 2.0 / 9.0, 2: 1.0 / 18.0, 3: 1.0 / 72.0}
    scaled = {n: [part * weight[n] for part in force] for n in weight}
    terms = [None] * 27
    for q in range(14, 27):
        c = components(q)
        total = None
        for i in range(3):
            if c[i] == 0:
                continue
            part = scaled[sum(1 for v in c if v != 0)][i]
            if total is None:
                total = part
            elif c[i] > 0:
                total = total + part
            else:
                total = total - part
        terms[q] = (total, 1)
        terms[26 - q] = (total, -1)
    return terms


def pushed(value, term):
    if term is None:
        return value
    return value + term[0] if term[1] > 0 else value - term[0]


def group_order(leaves):
    root = leaves * 5 // 8
    return [root] + [leaf for leaf in range(leaves) if leaf != root]


def bin_kernel(forces_hbm, dest_hbm, cells_hbm, sent_ref, forces_ref, dest_ref, cells_ref, sems):
    pairs = ((dest_hbm, dest_ref), (cells_hbm, cells_ref), (forces_hbm, forces_ref))
    copies = [pltpu.make_async_copy(a, b, sems.at[i]) for i, (a, b) in enumerate(pairs)]
    for each in copies:
        each.start()
    markers = cells_ref.shape[1]
    leaves = sent_ref.shape[0]
    root = leaves * 5 // 8
    highest = lax.Precision.HIGHEST
    earlier = (
        lax.broadcasted_iota(jnp.int32, (markers, markers), 0)
        < lax.broadcasted_iota(jnp.int32, (markers, markers), 1)
    ).astype(F32).astype(BF16)
    copies[0].wait()
    hot = []
    for t in range(2):
        row = dest_ref[t]
        row = jnp.where(row < root, row + 1, jnp.where(row == root, 0, row))
        leaf = lax.broadcasted_iota(jnp.int32, (leaves, markers), 0)
        hot.append((leaf == row).astype(F32))
    ahead = jnp.dot(
        jnp.concatenate(hot, axis=0).astype(BF16), earlier, preferred_element_type=F32
    )
    copies[1].wait()
    copies[2].wait()
    left, right = [], []
    for t in range(2):
        rank = jnp.sum(hot[t] * ahead[t * leaves : (t + 1) * leaves], axis=0, keepdims=True)
        rank = rank.astype(jnp.int32)
        third = rank // 16
        left.append(jnp.concatenate([jnp.where(third == r, hot[t], 0.0) for r in range(3)], axis=0))
        spot = lax.broadcasted_iota(jnp.int32, (16, markers), 0) == rank % 16
        rows = [cells_ref[t : t + 1, :].astype(F32)] + [forces_ref[c, t : t + 1, :] for c in range(3)]
        own = jnp.concatenate([jnp.where(spot, row, 0.0) for row in rows], axis=0)
        none = jnp.zeros_like(own)
        right.append(jnp.concatenate([own, none] if t == 0 else [none, own], axis=0))
    packed = lax.dot_general(
        jnp.concatenate(left, axis=1),
        jnp.concatenate(right, axis=1),
        (((1,), (1,)), ((), ())),
        precision=highest,
        preferred_element_type=F32,
    )
    for r in range(3):
        sent_ref[:, r, :] = packed[r * leaves : (r + 1) * leaves]


def first_kernel(rates_ref, after_ref, populations_ref, collided_ref):
    width = populations_ref.shape[1]
    base = pl.program_id(0) * width

    def plane(x, carry):
        result = collide(
            [populations_ref[q, x] for q in range(27)], lambda k: rates_ref[k], None
        )
        for q in range(27):
            collided_ref[q, base + x] = result[q]
        return carry

    lax.fori_loop(0, width, plane, 0)


def rows_by_value(received_ref):
    blocks = []
    for r in range(2):
        whole = received_ref[:, r, :]
        blocks += [whole[8 * b : 8 * b + 8] for b in range(4)]
    lane = lax.broadcasted_iota(jnp.int32, (8, 128), 1)
    for half in (4, 2, 1):
        low = (lane // (16 * half)) % 2 == 0
        for b in range(8):
            if b & half:
                continue
            first, second = blocks[b], blocks[b + half]
            blocks[b] = jnp.where(low, first, pltpu.roll(second, 16 * half, 1))
            blocks[b + half] = jnp.where(low, pltpu.roll(first, 128 - 16 * half, 1), second)
    last = received_ref[:, 2, :]
    tail = None
    for b in range(4):
        part = last[8 * b : 8 * b + 8]
        part = jnp.where(lane % 16 < 4, part, 0.0)
        if b:
            part = pltpu.roll(part, 4 * b, 1)
        tail = part if tail is None else tail + part
    sub = lax.broadcasted_iota(jnp.int32, (8, 128), 0)
    rows = []
    for v in range(8):
        spread = pltpu.roll(tail, 128 - 16 * v, 1) if v else tail
        spread = pltpu.roll(spread, 0, 1, stride=16, stride_axis=0)
        spread = jnp.where(lane // 16 == sub, spread, 0.0)
        rows.append((blocks[v], jnp.sum(spread, axis=0, keepdims=True)))
    return rows


def rows_of(height, sign):
    edge, inside = (height - 1, height - 2) if sign > 0 else (0, 1)
    return ((edge, 0, (0, sign)), (inside, 18, (sign,)))


def own_faces(collided_ref, field_ref, up_ref, down_ref):
    height = collided_ref.shape[2]
    for ref, sign in ((up_ref, 1), (down_ref, -1)):
        for z, first, kinds in rows_of(height, sign):
            terms = sources([field_ref[0, c, :, z, :] for c in range(3)])
            for order, cz in enumerate(kinds):
                for j in range(9):
                    q = 3 * j + cz + 1
                    ref[first + 9 * order + j] = pushed(collided_ref[q, :, z, :], terms[q])
        for c in range(3):
            ref[27 + c] = field_ref[1, c, :, height - 1 if sign > 0 else 0, :]


def deposit_kernel(
    parity_ref, received_ref, collided_ref, field_ref, a_ref, b_ref, up_ref, down_ref
):
    rows = rows_by_value(received_ref)
    index = lax.broadcasted_iota(jnp.int32, (128, 128), 0).astype(F32).astype(BF16)
    one, zero = jnp.ones((), BF16), jnp.zeros((), BF16)
    for t in range(2):
        values = rows[4 * t : 4 * t + 4]
        chunks = [[v[0][s : s + 1] for s in range(8)] + [v[1]] for v in values]
        outer, weighted = [], []
        for s in range(9):
            cell = chunks[0][s].astype(jnp.int32)
            outer.append(jnp.where(index == (cell // 128).astype(F32).astype(BF16), one, zero))
            inner = index == (cell % 128).astype(F32).astype(BF16)
            parts = []
            for c in range(3):
                amount = chunks[c + 1][s]
                big = amount.astype(BF16)
                small = (amount - big.astype(F32)).astype(BF16)
                parts.append((jnp.where(inner, big, zero), jnp.where(inner, small, zero)))
            weighted.append(
                jnp.concatenate([p[0] for p in parts] + [p[1] for p in parts], axis=0)
            )
        field = lax.dot_general(
            jnp.concatenate(outer, axis=1),
            jnp.concatenate(weighted, axis=1),
            (((1,), (1,)), ((), ())),
            preferred_element_type=F32,
        )
        for c in range(3):
            whole = field[:, 128 * c : 128 * c + 128] + field[:, 384 + 128 * c : 512 + 128 * c]
            field_ref[t, c] = whole.reshape(field_ref.shape[2:])
    last = collided_ref.shape[1] - 1

    def layers(ref, sign, edge, inside):
        terms = sources([field_ref[0, c, edge] for c in range(3)])
        for n in range(18):
            q = 9 + n if n < 9 else 9 + 9 * sign + n - 9
            ref[n] = pushed(collided_ref[q, edge], terms[q])
        terms = sources([field_ref[0, c, inside] for c in range(3)])
        for n in range(9):
            q = 9 + 9 * sign + n
            ref[18 + n] = pushed(collided_ref[q, inside], terms[q])
        for c in range(3):
            ref[27 + c] = field_ref[1, c, edge]

    @pl.when(parity_ref[0] == 0)
    def _():
        layers(a_ref, 1, last, last - 1)
        layers(b_ref, -1, 0, 1)

    @pl.when(parity_ref[0] != 0)
    def _():
        layers(b_ref, 1, last, last - 1)
        layers(a_ref, -1, 0, 1)

    own_faces(collided_ref, field_ref, up_ref, down_ref)


def corner_at(place, number):
    return place // 2, pl.ds(4 * (place % 2) + number, 1)


def corner_kernel(parity_ref, a_ref, b_ref, after_ref, halo_ref, up_ref, down_ref):
    @pl.when(parity_ref[0] == 0)
    def _():
        halo_ref[0] = b_ref[...]
        halo_ref[1] = a_ref[...]

    @pl.when(parity_ref[0] != 0)
    def _():
        halo_ref[0] = a_ref[...]
        halo_ref[1] = b_ref[...]

    height = a_ref.shape[1]
    for ref, sign in ((up_ref, 1), (down_ref, -1)):

        def put(place, number, side, layer, z):
            tile, row = corner_at(place, number)
            ref[tile, row, :] = halo_ref[side, layer, pl.ds(z, 1), :]

        for z, first, kinds in rows_of(height, sign):
            for order, cz in enumerate(kinds):
                for j in range(9):
                    place = first + 9 * order + j
                    cx = j // 3 - 1
                    n = 3 * (j % 3) + cz + 1
                    for side, toward, near, far in ((0, 1, 1, 0), (1, -1, 2, 3)):
                        if cx == 0:
                            put(place, near, side, n, z)
                        if cx == toward:
                            put(place, near, side, 9 + n, z)
                            put(place, far, side, 18 + n, z)
        edge = height - 1 if sign > 0 else 0
        for c in range(3):
            put(27 + c, 1, 0, 27 + c, edge)
            put(27 + c, 2, 1, 27 + c, edge)


def moved(tile, q, low_row, high_row):
    _, cy, cz = components(q)
    height = tile.shape[0]
    if cz:
        sub = lax.broadcasted_iota(jnp.int32, tile.shape, 0)
        if cz > 0:
            tile = jnp.where(sub == 0, low_row(), pltpu.roll(tile, 1, 0))
        else:
            tile = jnp.where(sub == height - 1, high_row(), pltpu.roll(tile, height - 1, 0))
    return pltpu.roll(tile, cy % 128, 1) if cy else tile


def edge_rows(got, sent, toward, start, force, rate):
    values = []
    for q in range(27):
        cx, cy, cz = components(q)
        j = q // 3
        where = pl.ds(start - cx, 8)
        if cz == toward:
            row = got(18 + j, where)
        elif cz == 0:
            row = got(j, where)
        else:
            row = sent(9 + j, where)
        values.append(pltpu.roll(row, cy % 128, 1) if cy else row)
    after = collide(values, rate, force)
    return [after[3 * j + toward + 1] for j in range(9)]


def second(x, force, rate, state, ring, result):
    after = collide([state[q, x] for q in range(27)], rate, force)
    for q in range(27):
        j = q // 3
        result[q, x + q // 9 - 1] = moved(
            after[q],
            q,
            lambda: ring[0, j, pl.ds(x, 1), :],
            lambda: ring[1, j, pl.ds(x, 1), :],
        )


def write_out(result, out_ref, sem, plane, count):
    return pltpu.make_async_copy(
        result.at[:, pl.ds(2 + plane, count)], out_ref.at[:, pl.ds(plane, count)], sem
    )


def planes(first, last, rate, field_ref, state, ring, result, out_ref, sems):
    def plane(x, carry):
        second(x + 2, [field_ref[1, c, x] for c in range(3)], rate, state, ring, result)
        return carry

    copies = []
    done = first
    for place in range(max(2, first - 1), last - 2, 2):
        lax.fori_loop(done, place + 3, plane, 0)
        done = place + 3
        copies.append(write_out(result, out_ref, sems.at[len(copies)], place, 2))
        copies[-1].start()
    for each in copies:
        each.wait()


def inner_kernel(
    rates_ref, collided_ref, field_ref, up_ref, down_ref, low_ref, high_ref,
    out_ref, state, result, ring, sems,
):
    width = collided_ref.shape[1]
    rate = lambda k: rates_ref[k]

    def own(x, carry):
        terms = sources([field_ref[0, c, x] for c in range(3)])
        for q in range(27):
            place = 9 + q // 3
            tile = pushed(collided_ref[q, x], terms[q])
            state[q, x + 2 + q // 9 - 1] = moved(
                tile,
                q,
                lambda: low_ref[place, pl.ds(x, 1), :],
                lambda: high_ref[place, pl.ds(x, 1), :],
            )
        return carry

    lax.fori_loop(0, width, own, 0)
    for side, got, sent, toward in ((0, low_ref, down_ref, 1), (1, high_ref, up_ref, -1)):

        def edge(block, carry, side=side, got=got, sent=sent, toward=toward):
            start = 1 + (width - 10) * block
            force = [got[27 + c, pl.ds(start, 8), :] for c in range(3)]
            rows = edge_rows(
                lambda place, where: got[place, where, :],
                lambda place, where: sent[place, where, :],
                toward, start, force, rate,
            )
            for j in range(9):
                ring[side, j, pl.ds(start + 2, 8), :] = rows[j]
            return carry

        lax.fori_loop(0, 2, edge, 0)
    planes(1, SPLIT, rate, field_ref, state, ring, result, out_ref, sems)


def more_kernel(
    rates_ref, state, field_ref, ring, result_in, out_in, out_ref, result, sems
):
    width = field_ref.shape[2]
    rate = lambda k: rates_ref[k]
    planes(SPLIT, width - 1, rate, field_ref, state, ring, result, out_ref, sems)


def outer_kernel(
    rates_ref, halo_ref, state_in, result_in, out_in, field_ref,
    up_ref, down_ref, low_ref, high_ref,
    up_corner, down_corner, low_corner, high_corner,
    out_ref, state, result, got, sent, ring, sems,
):
    width = field_ref.shape[2]
    rate = lambda k: rates_ref[k]
    columns = (0, 1, width + 2, width + 3)
    for side, toward, near in ((0, 1, 1), (1, -1, width + 2)):
        for n in range(27):
            q = 9 + n if n < 9 else 9 + 9 * toward + n % 9
            column = near if n < 18 else near - toward
            place = 9 + q // 3
            tile, row = corner_at(place, columns.index(column))
            state[q, column + q // 9 - 1] = moved(
                halo_ref[side, n],
                q,
                lambda: low_corner[tile, row, :],
                lambda: high_corner[tile, row, :],
            )

    def gather(target, place, own, corner, source):
        target[place, pl.ds(2, width), :] = own[source]
        for number, column in enumerate(columns):
            tile, row = corner_at(source, number)
            target[place, pl.ds(column, 1), :] = corner[tile, row, :]

    sides = (
        (0, low_ref, low_corner, down_ref, down_corner, 1),
        (1, high_ref, high_corner, up_ref, up_corner, -1),
    )
    for side, mine, corner, left, left_corner, toward in sides:
        for place in list(range(9)) + list(range(18, 30)):
            gather(got.at[side], place, mine, corner, place)
        for j in range(9):
            gather(sent.at[side], j, left, left_corner, 9 + j)

        def edge(block, carry, side=side, toward=toward):
            start = 1 + (width - 6) * block
            force = [got[side, 27 + c, pl.ds(start, 8), :] for c in range(3)]
            rows = edge_rows(
                lambda place, where: got[side, place, where, :],
                lambda place, where: sent[side, place - 9, where, :],
                toward, start, force, rate,
            )
            for j in range(9):
                ring[side, j, pl.ds(start, 8), :] = rows[j]
            return carry

        lax.fori_loop(0, 2, edge, 0)

    second(1, [halo_ref[0, 27 + c] for c in range(3)], rate, state, ring, result)
    second(2, [field_ref[1, c, 0] for c in range(3)], rate, state, ring, result)
    first = write_out(result, out_ref, sems.at[0], 0, 2)
    first.start()
    second(width + 1, [field_ref[1, c, width - 1] for c in range(3)], rate, state, ring, result)
    second(width + 2, [halo_ref[1, 27 + c] for c in range(3)], rate, state, ring, result)
    last = write_out(result, out_ref, sems.at[1], width - 2, 2)
    last.start()
    first.wait()
    last.wait()


def cost(flops, moved):
    return pl.CostEstimate(flops=flops, bytes_accessed=moved, transcendentals=0)


def body(populations, relax_rates, marker_forces, marker_dest, marker_cells):
    width, height, length = populations.shape[1:]
    leaves = lax.axis_size("leaf")
    spans = lax.axis_size("span")
    markers = marker_cells.shape[1]
    held = functools.partial(pltpu.with_memory_space_constraint, memory_space=pltpu.VMEM)
    far = functools.partial(pltpu.with_memory_space_constraint, memory_space=pltpu.HBM)
    near = lambda *shape: pltpu.VMEM(shape, F32)
    sent = pl.pallas_call(
        bin_kernel,
        out_shape=near(leaves, 3, 128),
        in_specs=[HBM] * 3,
        out_specs=WHOLE,
        scratch_shapes=[
            pltpu.VMEM((3, 2, markers), F32),
            pltpu.VMEM((2, 1, markers), jnp.int32),
            pltpu.VMEM((2, markers), jnp.int32),
            pltpu.SemaphoreType.DMA((3,)),
        ],
        compiler_params=params(16),
        name="bin_markers",
    )(
        far(jnp.transpose(marker_forces, (1, 0, 2))),
        far(jnp.transpose(marker_dest, (0, 2, 1))),
        far(marker_cells),
    )
    received = lax.all_to_all(
        sent, "leaf", 0, 0, tiled=True, axis_index_groups=[group_order(leaves)]
    )
    block = 2
    collided = pl.pallas_call(
        first_kernel,
        grid=(width // block,),
        out_shape=near(*populations.shape),
        in_specs=[
            SCALARS,
            HBM,
            pl.BlockSpec((27, block, height, length), lambda i: (0, i, 0, 0)),
        ],
        out_specs=WHOLE,
        compiler_params=params(16),
        cost_estimate=cost(27 * 12 * width * height * length, 8 * populations.size),
        name="collide_first",
    )(relax_rates, sent, populations)
    parity = lax.rem(lax.axis_index("span"), 2).astype(jnp.int32).reshape(1)
    layer = near(30, height, length)
    own = near(30, width, length)
    field, a_sent, b_sent, up, down = pl.pallas_call(
        deposit_kernel,
        out_shape=[near(2, 3, width, height, length), layer, layer, own, own],
        in_specs=[SCALARS, WHOLE, WHOLE],
        out_specs=[WHOLE] * 5,
        compiler_params=params(24),
        name="deposit",
    )(parity, held(received), held(collided))
    a_pairs = [(s, s ^ 1) for s in range(spans)]
    b_pairs = [(s, (s + 1 if s % 2 else s - 1) % spans) for s in range(spans)]
    b_got = lax.ppermute(b_sent, "span", b_pairs)
    a_got = lax.ppermute(a_sent, "span", a_pairs)
    face = near(30, 24, length)
    upward = [(l, (l + 1) % leaves) for l in range(leaves)]
    downward = [(l, (l - 1) % leaves) for l in range(leaves)]
    low = lax.ppermute(up, "leaf", upward)
    high = lax.ppermute(down, "leaf", downward)
    padded = near(27, PLANES, height, length)
    final = pltpu.HBM(populations.shape, F32)
    faces = [held(each) for each in (up, down, low, high)]
    work = 27 * 12 * width * height * length
    out, state, result, ring = pl.pallas_call(
        inner_kernel,
        out_shape=[final, padded, padded, near(2, 9, 24, length)],
        in_specs=[SCALARS] + [WHOLE] * 6,
        out_specs=[HBM] + [WHOLE] * 3,
        scratch_shapes=[pltpu.SemaphoreType.DMA((SPLIT // 2,))],
        compiler_params=params(16),
        cost_estimate=cost(work, 4 * populations.size),
        name="first_planes",
    )(relax_rates, held(collided), held(field), *faces)
    corner = near(15, 8, length)
    halo, up_corner, down_corner = pl.pallas_call(
        corner_kernel,
        out_shape=[near(2, 30, height, length), corner, corner],
        in_specs=[SCALARS] + [WHOLE] * 2 + [HBM],
        out_specs=[WHOLE] * 3,
        compiler_params=params(16),
        name="corners",
    )(parity, held(a_got), held(b_got), ring)
    low_corner = lax.ppermute(up_corner, "leaf", upward)
    high_corner = lax.ppermute(down_corner, "leaf", downward)
    out, result = pl.pallas_call(
        more_kernel,
        out_shape=[final, padded],
        in_specs=[SCALARS] + [WHOLE] * 4 + [HBM],
        out_specs=[HBM, WHOLE],
        input_output_aliases={4: 1, 5: 0},
        scratch_shapes=[pltpu.SemaphoreType.DMA((width // 2,))],
        compiler_params=params(16),
        cost_estimate=cost(work, 4 * populations.size),
        name="more_planes",
    )(relax_rates, held(state), held(field), held(ring), held(result), far(out))
    corners = [held(each) for each in (up_corner, down_corner, low_corner, high_corner)]
    return pl.pallas_call(
        outer_kernel,
        out_shape=[final, padded, padded],
        in_specs=[SCALARS, WHOLE, WHOLE, WHOLE, HBM] + [WHOLE] * 9,
        out_specs=[HBM, WHOLE, WHOLE],
        input_output_aliases={2: 1, 3: 2, 4: 0},
        scratch_shapes=[
            pltpu.VMEM((2, 30, 24, length), F32),
            pltpu.VMEM((2, 9, 24, length), F32),
            pltpu.VMEM((2, 9, 24, length), F32),
            pltpu.SemaphoreType.DMA((2,)),
        ],
        compiler_params=params(16),
        name="outer_planes",
    )(relax_rates, held(halo), held(state), held(result), far(out), held(field), *faces, *corners)[0]


def solution(mesh):
    placed = (
        P(None, "span", "leaf", None),
        P(),
        P(None, None, ("span", "leaf")),
        P(None, ("span", "leaf"), None),
        P(None, ("span", "leaf")),
    )
    return jax.shard_map(
        body, mesh=mesh, in_specs=placed, out_specs=P(None, "span", "leaf", None), check_vma=False
    )
```

```python
import functools
import jax
import jax.numpy as jnp
import numpy as np
from jax import lax
from jax.experimental import pallas as pl
from jax.experimental.pallas import tpu as pltpu
from jax.sharding import PartitionSpec as P

F32 = jnp.float32
BF16 = jnp.bfloat16
SPLIT = 7
PLANES = 20
WHOLE = pl.BlockSpec(memory_space=pltpu.VMEM)
SCALARS = pl.BlockSpec(memory_space=pltpu.SMEM)
HBM = pl.BlockSpec(memory_space=pl.ANY)


def params(mib):
    return pltpu.CompilerParams(vmem_limit_bytes=mib * 2**20)


def components(q):
    return q // 9 - 1, (q // 3) % 3 - 1, q % 3 - 1


def transform(values, step):
    values = list(values)
    for stride in (9, 3, 1):
        for q in range(27):
            if (q // stride) % 3 == 0:
                triple = (q, q + stride, q + 2 * stride)
                for place, value in zip(triple, step(*[values[i] for i in triple])):
                    values[place] = value
    return values


def to_moments(low, middle, high):
    both = low + high
    return both + middle, high - low, both


def from_moments(zeroth, first, second):
    return second - first, zeroth - second, second + first


def collide(populations, rate, force):
    moments = transform(populations, to_moments)
    density = moments[0]
    momentum = (moments[9], moments[3], moments[1])
    velocity = [part * (1.0 / 27.0) for part in momentum]
    flux = [27.0 * part for part in velocity]
    energy = [3.0 * f * v for f, v in zip(flux, velocity)]
    cross = {}
    for i in range(3):
        for j in range(i + 1, 3):
            cross[i, j] = flux[i] * velocity[j]
    relaxed = []
    for k in range(27):
        powers = (k // 9, (k // 3) % 3, k % 3)
        odd = [i for i in range(3) if powers[i] == 1]
        squares = [i for i in range(3) if powers[i] == 2]
        share = 3.0 ** -len(squares)
        if len(odd) == 0:
            level = density
            for i in squares:
                level = level + energy[i]
        elif len(odd) == 1:
            level = flux[odd[0]]
        elif len(odd) == 2:
            level = cross[odd[0], odd[1]]
        else:
            level = None
        if level is not None and squares:
            level = level * share
        gap = moments[k] if level is None else moments[k] - level
        value = moments[k] - rate(k) * gap
        if force is not None and len(odd) == 1:
            push = force[odd[0]]
            value = value + (push * share if squares else push)
        relaxed.append(value)
    result = transform(relaxed, from_moments)
    scaled = []
    for q in range(27):
        moving = sum(1 for c in components(q) if c != 0)
        scaled.append(result[q] * 0.5**moving if moving else result[q])
    return scaled


def sources(force):
    weight = {1: 2.0 / 9.0, 2: 1.0 / 18.0, 3: 1.0 / 72.0}
    scaled = {n: [part * weight[n] for part in force] for n in weight}
    terms = [None] * 27
    for q in range(14, 27):
        c = components(q)
        total = None
        for i in range(3):
            if c[i] == 0:
                continue
            part = scaled[sum(1 for v in c if v != 0)][i]
            if total is None:
                total = part
            elif c[i] > 0:
                total = total + part
            else:
                total = total - part
        terms[q] = (total, 1)
        terms[26 - q] = (total, -1)
    return terms


def pushed(value, term):
    if term is None:
        return value
    return value + term[0] if term[1] > 0 else value - term[0]


def group_order(leaves):
    root = leaves * 5 // 8
    return [root] + [leaf for leaf in range(leaves) if leaf != root]


def bin_kernel(forces_hbm, dest_hbm, cells_hbm, sent_ref, forces_ref, dest_ref, cells_ref, sems):
    pairs = ((dest_hbm, dest_ref), (cells_hbm, cells_ref), (forces_hbm, forces_ref))
    copies = [pltpu.make_async_copy(a, b, sems.at[i]) for i, (a, b) in enumerate(pairs)]
    for each in copies:
        each.start()
    markers = cells_ref.shape[1]
    leaves = sent_ref.shape[0]
    root = leaves * 5 // 8
    earlier = (
        lax.broadcasted_iota(jnp.int32, (markers, markers), 0)
        < lax.broadcasted_iota(jnp.int32, (markers, markers), 1)
    ).astype(F32).astype(BF16)
    copies[0].wait()
    hot = []
    for t in range(2):
        row = dest_ref[t]
        row = jnp.where(row < root, row + 1, jnp.where(row == root, 0, row))
        leaf = lax.broadcasted_iota(jnp.int32, (leaves, markers), 0)
        hot.append((leaf == row).astype(F32))
    ahead = jnp.dot(
        jnp.concatenate(hot, axis=0).astype(BF16), earlier, preferred_element_type=F32
    )
    copies[1].wait()
    copies[2].wait()
    left, right = [], []
    for t in range(2):
        rank = jnp.sum(hot[t] * ahead[t * leaves : (t + 1) * leaves], axis=0, keepdims=True)
        rank = rank.astype(jnp.int32)
        third = rank // 16
        left.append(jnp.concatenate([jnp.where(third == r, hot[t], 0.0) for r in range(3)], axis=0))
        spot = lax.broadcasted_iota(jnp.int32, (16, markers), 0) == rank % 16
        rows = [cells_ref[t : t + 1, :].astype(F32)] + [forces_ref[c, t : t + 1, :] for c in range(3)]
        own = jnp.concatenate([jnp.where(spot, row, 0.0) for row in rows], axis=0)
        none = jnp.zeros_like(own)
        right.append(jnp.concatenate([own, none] if t == 0 else [none, own], axis=0))
    values = jnp.concatenate(right, axis=1)
    parts = []
    for _ in range(3):
        part = values.astype(BF16)
        parts.append(part)
        values = values - part.astype(F32)
    packed = lax.dot_general(
        jnp.concatenate(left, axis=1).astype(BF16),
        jnp.concatenate(parts, axis=0),
        (((1,), (1,)), ((), ())),
        preferred_element_type=F32,
    )
    packed = packed[:, :128] + packed[:, 128:256] + packed[:, 256:]
    for r in range(3):
        sent_ref[:, 0, 128 * r : 128 * r + 128] = packed[r * leaves : (r + 1) * leaves]


def first_kernel(rates_ref, after_ref, populations_ref, collided_ref):
    width = populations_ref.shape[1]
    base = pl.program_id(0) * width

    def plane(x, carry):
        result = collide(
            [populations_ref[q, x] for q in range(27)], lambda k: rates_ref[k], None
        )
        for q in range(27):
            collided_ref[q, base + x] = result[q]
        return carry

    lax.fori_loop(0, width, plane, 0)


def rows_by_value(received_ref):
    blocks = []
    for r in range(2):
        whole = received_ref[:, 0, 128 * r : 128 * r + 128]
        blocks += [whole[8 * b : 8 * b + 8] for b in range(4)]
    lane = lax.broadcasted_iota(jnp.int32, (8, 128), 1)
    for half in (4, 2, 1):
        low = (lane // (16 * half)) % 2 == 0
        for b in range(8):
            if b & half:
                continue
            first, second = blocks[b], blocks[b + half]
            blocks[b] = jnp.where(low, first, pltpu.roll(second, 16 * half, 1))
            blocks[b + half] = jnp.where(low, pltpu.roll(first, 128 - 16 * half, 1), second)
    last = received_ref[:, 0, 256:384]
    tail = None
    for b in range(4):
        part = last[8 * b : 8 * b + 8]
        part = jnp.where(lane % 16 < 4, part, 0.0)
        if b:
            part = pltpu.roll(part, 4 * b, 1)
        tail = part if tail is None else tail + part
    sub = lax.broadcasted_iota(jnp.int32, (8, 128), 0)
    rows = []
    for v in range(8):
        spread = pltpu.roll(tail, 128 - 16 * v, 1) if v else tail
        spread = pltpu.roll(spread, 0, 1, stride=16, stride_axis=0)
        spread = jnp.where(lane // 16 == sub, spread, 0.0)
        rows.append((blocks[v], jnp.sum(spread, axis=0, keepdims=True)))
    return rows


def rows_of(height, sign):
    edge, inside = (height - 1, height - 2) if sign > 0 else (0, 1)
    return ((edge, 0, (0, sign)), (inside, 18, (sign,)))


def own_faces(collided_ref, field_ref, up_ref, down_ref):
    height = collided_ref.shape[2]
    for ref, sign in ((up_ref, 1), (down_ref, -1)):
        for z, first, kinds in rows_of(height, sign):
            terms = sources([field_ref[0, c, :, z, :] for c in range(3)])
            for order, cz in enumerate(kinds):
                for j in range(9):
                    q = 3 * j + cz + 1
                    ref[first + 9 * order + j] = pushed(collided_ref[q, :, z, :], terms[q])
        for c in range(3):
            ref[27 + c] = field_ref[1, c, :, height - 1 if sign > 0 else 0, :]


def deposit_kernel(received_ref, collided_ref, field_ref, up_ref, down_ref):
    rows = rows_by_value(received_ref)
    index = lax.broadcasted_iota(jnp.int32, (128, 128), 0).astype(F32).astype(BF16)
    one, zero = jnp.ones((), BF16), jnp.zeros((), BF16)
    for t in range(2):
        values = rows[4 * t : 4 * t + 4]
        chunks = [[v[0][s : s + 1] for s in range(8)] + [v[1]] for v in values]
        outer, weighted = [], []
        for s in range(9):
            cell = chunks[0][s].astype(jnp.int32)
            outer.append(jnp.where(index == (cell // 128).astype(F32).astype(BF16), one, zero))
            inner = index == (cell % 128).astype(F32).astype(BF16)
            parts = []
            for c in range(3):
                amount = chunks[c + 1][s]
                big = amount.astype(BF16)
                small = (amount - big.astype(F32)).astype(BF16)
                parts.append((jnp.where(inner, big, zero), jnp.where(inner, small, zero)))
            weighted.append(
                jnp.concatenate([p[0] for p in parts] + [p[1] for p in parts], axis=0)
            )
        field = lax.dot_general(
            jnp.concatenate(weighted, axis=1),
            jnp.concatenate(outer, axis=1),
            (((1,), (1,)), ((), ())),
            preferred_element_type=F32,
        )
        for c in range(3):
            whole = field[128 * c : 128 * c + 128] + field[384 + 128 * c : 512 + 128 * c]
            field_ref[t, c] = whole.T.reshape(field_ref.shape[2:])
    own_faces(collided_ref, field_ref, up_ref, down_ref)


def corner_at(place, number):
    return place // 2, pl.ds(4 * (place % 2) + number, 1)


def side_kernel(parity_ref, collided_ref, field_ref, after_ref, low_ref, high_ref, a_ref, b_ref):
    last = collided_ref.shape[1] - 1

    def layers(ref, sign, edge, inside):
        def put(n, number, got, place, x):
            tile, row = corner_at(n, number)
            ref[30 + tile, row, :] = got[place, pl.ds(x, 1), :]

        for first, count, x in ((0, 18, edge), (18, 9, inside)):
            terms = sources([field_ref[0, c, x] for c in range(3)])
            for n in range(first, first + count):
                q = 9 + n if n < 9 else 9 + 9 * sign + n % 9
                j, cz = q // 3, q % 3 - 1
                ref[n] = pushed(collided_ref[q, x], terms[q])
                if cz >= 0:
                    put(n, 1, low_ref, 9 * cz + j, x)
                if cz <= 0:
                    put(n, 2, high_ref, -9 * cz + j, x)
                if cz > 0:
                    put(n, 0, low_ref, 18 + j, x)
                if cz < 0:
                    put(n, 3, high_ref, 18 + j, x)
        for c in range(3):
            ref[27 + c] = field_ref[1, c, edge]
            put(27 + c, 1, low_ref, 27 + c, edge)
            put(27 + c, 2, high_ref, 27 + c, edge)

    @pl.when(parity_ref[0] == 0)
    def _():
        layers(a_ref, 1, last, last - 1)
        layers(b_ref, -1, 0, 1)

    @pl.when(parity_ref[0] != 0)
    def _():
        layers(b_ref, 1, last, last - 1)
        layers(a_ref, -1, 0, 1)


def corner_kernel(
    parity_ref, a_ref, b_ref, after_ref,
    halo_ref, up_ref, down_ref, low_ref, high_ref,
):
    @pl.when(parity_ref[0] == 0)
    def _():
        halo_ref[0] = b_ref[...]
        halo_ref[1] = a_ref[...]

    @pl.when(parity_ref[0] != 0)
    def _():
        halo_ref[0] = a_ref[...]
        halo_ref[1] = b_ref[...]

    height = a_ref.shape[1]

    def columns(place, cz, load, ref):
        cx = (place % 9) // 3 - 1
        n = 3 * (place % 3) + cz + 1
        for side, toward, near, far in ((0, 1, 1, 0), (1, -1, 2, 3)):
            wanted = [(near, n)] if cx == 0 else []
            if cx == toward:
                wanted = [(near, 9 + n), (far, 18 + n)]
            for number, layer in wanted:
                tile, row = corner_at(place, number)
                ref[tile, row, :] = load(side, layer)

    def outside(number):
        def load(side, layer):
            tile, row = corner_at(layer, number)
            return halo_ref[side, 30 + tile, row, :]

        return load

    for ref, own_ref, sign, first, z in (
        (low_ref, down_ref, 1, 1, 0),
        (high_ref, up_ref, -1, 2, height - 1),
    ):
        for j in range(9):
            columns(j, 0, outside(first), ref)
            columns(9 + j, sign, outside(first), ref)
            columns(18 + j, sign, outside(first - sign), ref)
            columns(9 + j, -sign, lambda side, n: halo_ref[side, n, pl.ds(z, 1), :], own_ref)
        for c in range(3):
            for side, number in ((0, 1), (1, 2)):
                tile, row = corner_at(27 + c, number)
                ref[tile, row, :] = outside(first)(side, 27 + c)


def moved(tile, q, low_row, high_row):
    _, cy, cz = components(q)
    height = tile.shape[0]
    if cz:
        sub = lax.broadcasted_iota(jnp.int32, tile.shape, 0)
        if cz > 0:
            tile = jnp.where(sub == 0, low_row(), pltpu.roll(tile, 1, 0))
        else:
            tile = jnp.where(sub == height - 1, high_row(), pltpu.roll(tile, height - 1, 0))
    return pltpu.roll(tile, cy % 128, 1) if cy else tile


def edge_rows(got, sent, toward, start, force, rate):
    values = []
    for q in range(27):
        cx, cy, cz = components(q)
        j = q // 3
        where = pl.ds(start - cx, 8)
        if cz == toward:
            row = got(18 + j, where)
        elif cz == 0:
            row = got(j, where)
        else:
            row = sent(9 + j, where)
        values.append(pltpu.roll(row, cy % 128, 1) if cy else row)
    after = collide(values, rate, force)
    return [after[3 * j + toward + 1] for j in range(9)]


def second(x, force, rate, state, ring, result, row=None):
    row = x if row is None else row
    after = collide([state[q, x] for q in range(27)], rate, force)
    for q in range(27):
        j = q // 3
        result[q, x + q // 9 - 1] = moved(
            after[q],
            q,
            lambda: ring[0, j, pl.ds(row, 1), :],
            lambda: ring[1, j, pl.ds(row, 1), :],
        )


def write_out(result, out_ref, sem, plane, count):
    return pltpu.make_async_copy(
        result.at[:, pl.ds(2 + plane, count)], out_ref.at[:, pl.ds(plane, count)], sem
    )


def planes(first, last, rate, field_ref, state, ring, result):
    def plane(x, carry):
        second(x + 2, [field_ref[1, c, x] for c in range(3)], rate, state, ring, result)
        return carry

    lax.fori_loop(first, last, plane, 0)


def stream_kernel(collided_ref, field_ref, state):
    def own(x, carry):
        terms = sources([field_ref[0, c, x] for c in range(3)])
        for q in range(27):
            cx, cy, cz = components(q)
            tile = pushed(collided_ref[q, x], terms[q])
            if cz:
                tile = pltpu.roll(tile, cz % tile.shape[0], 0)
            if cy:
                tile = pltpu.roll(tile, cy % 128, 1)
            state[q, x + 2 + cx] = tile
        return carry

    lax.fori_loop(0, collided_ref.shape[1], own, 0)


def inner_kernel(
    rates_ref, state_in, field_ref, up_ref, down_ref, low_ref, high_ref,
    state, result, ring,
):
    width, height = field_ref.shape[2:4]
    rate = lambda k: rates_ref[k]
    for q in range(27):
        cx, cy, cz = components(q)
        if cz == 0:
            continue
        got, z = (low_ref, 0) if cz > 0 else (high_ref, height - 1)
        rows = got[9 + q // 3]
        state[q, pl.ds(2 + cx, width), z, :] = pltpu.roll(rows, cy % 128, 1) if cy else rows
    for side, got, sent, toward in ((0, low_ref, down_ref, 1), (1, high_ref, up_ref, -1)):

        def edge(block, carry, side=side, got=got, sent=sent, toward=toward):
            start = 1 + (width - 10) * block
            force = [got[27 + c, pl.ds(start, 8), :] for c in range(3)]
            rows = edge_rows(
                lambda place, where: got[place, where, :],
                lambda place, where: sent[place, where, :],
                toward, start, force, rate,
            )
            for j in range(9):
                ring[side, j, pl.ds(start + 2, 8), :] = rows[j]
            return carry

        lax.fori_loop(0, 2, edge, 0)
    planes(1, SPLIT, rate, field_ref, state, ring, result)


def more_kernel(rates_ref, state, field_ref, ring, result_in, out_ref, result, sems):
    width = field_ref.shape[2]
    rate = lambda k: rates_ref[k]
    copies = [write_out(result, out_ref, sems.at[0], 2, SPLIT - 3)]
    copies[0].start()
    done = SPLIT
    for place in range(SPLIT - 1, width - 4, 2):
        planes(done, place + 3, rate, field_ref, state, ring, result)
        done = place + 3
        copies.append(write_out(result, out_ref, sems.at[len(copies)], place, 2))
        copies[-1].start()
    planes(done, width - 1, rate, field_ref, state, ring, result)
    for each in copies:
        each.wait()


def outer_kernel(
    rates_ref, halo_ref, state_in, result_in, out_in, field_ref,
    up_ref, down_ref, low_ref, high_ref,
    up_corner, down_corner, low_corner, high_corner,
    out_ref, state, result, got, sent, ring, sems,
):
    width = field_ref.shape[2]
    rate = lambda k: rates_ref[k]
    ready = write_out(result, out_ref, sems.at[2], width - 4, 2)
    ready.start()
    columns = (0, 1, width + 2, width + 3)
    for side, toward, near in ((0, 1, 1), (1, -1, width + 2)):
        for n in range(27):
            q = 9 + n if n < 9 else 9 + 9 * toward + n % 9
            column = near if n < 18 else near - toward
            place = 9 + q // 3
            tile, row = corner_at(place, columns.index(column))
            state[q, column + q // 9 - 1] = moved(
                halo_ref[side, n],
                q,
                lambda: low_corner[tile, row, :],
                lambda: high_corner[tile, row, :],
            )

    def gather(target, place, own, corner, source):
        tile, row = source // 2, 4 * (source % 2)
        target[place, pl.ds(0, 2), :] = corner[tile, pl.ds(row, 2), :]
        target[place, pl.ds(2, 2), :] = own[source, pl.ds(0, 2), :]
        target[place, pl.ds(4, 2), :] = own[source, pl.ds(width - 2, 2), :]
        target[place, pl.ds(6, 2), :] = corner[tile, pl.ds(row + 2, 2), :]

    sides = (
        (0, low_ref, low_corner, down_ref, down_corner, 1),
        (1, high_ref, high_corner, up_ref, up_corner, -1),
    )
    for side, mine, corner, left, left_corner, toward in sides:
        for place in list(range(9)) + list(range(18, 30)):
            gather(got.at[side], place, mine, corner, place)
        for j in range(9):
            gather(sent.at[side], j, left, left_corner, 9 + j)
        values = []
        for q in range(27):
            cx, cy, cz = components(q)
            j = q // 3
            if cz == toward:
                row = got[side, 18 + j]
            elif cz == 0:
                row = got[side, j]
            else:
                row = sent[side, j]
            if cx:
                row = pltpu.roll(row, cx % 8, 0)
            values.append(pltpu.roll(row, cy % 128, 1) if cy else row)
        after = collide(values, rate, [got[side, 27 + c] for c in range(3)])
        for j in range(9):
            ring[side, j] = after[3 * j + toward + 1]

    def plane(x, row, force):
        second(x, force, rate, state, ring, result, row)

    plane(1, 1, [halo_ref[0, 27 + c] for c in range(3)])
    plane(2, 2, [field_ref[1, c, 0] for c in range(3)])
    first = write_out(result, out_ref, sems.at[0], 0, 2)
    first.start()
    plane(width + 1, 5, [field_ref[1, c, width - 1] for c in range(3)])
    plane(width + 2, 6, [halo_ref[1, 27 + c] for c in range(3)])
    last = write_out(result, out_ref, sems.at[1], width - 2, 2)
    last.start()
    ready.wait()
    first.wait()
    last.wait()


def cost(flops, moved):
    return pl.CostEstimate(flops=flops, bytes_accessed=moved, transcendentals=0)


def body(populations, relax_rates, marker_forces, marker_dest, marker_cells):
    width, height, length = populations.shape[1:]
    leaves = lax.axis_size("leaf")
    spans = lax.axis_size("span")
    markers = marker_cells.shape[1]
    held = functools.partial(pltpu.with_memory_space_constraint, memory_space=pltpu.VMEM)
    far = functools.partial(pltpu.with_memory_space_constraint, memory_space=pltpu.HBM)
    near = lambda *shape: pltpu.VMEM(shape, F32)
    sent = pl.pallas_call(
        bin_kernel,
        out_shape=near(leaves, 1, 384),
        in_specs=[HBM] * 3,
        out_specs=WHOLE,
        scratch_shapes=[
            pltpu.VMEM((3, 2, markers), F32),
            pltpu.VMEM((2, 1, markers), jnp.int32),
            pltpu.VMEM((2, markers), jnp.int32),
            pltpu.SemaphoreType.DMA((3,)),
        ],
        compiler_params=params(16),
        name="bin_markers",
    )(
        far(jnp.transpose(marker_forces, (1, 0, 2))),
        far(jnp.transpose(marker_dest, (0, 2, 1))),
        far(marker_cells),
    )
    received = lax.all_to_all(
        sent, "leaf", 0, 0, tiled=True, axis_index_groups=[group_order(leaves)]
    )
    block = 2
    collided = pl.pallas_call(
        first_kernel,
        grid=(width // block,),
        out_shape=near(*populations.shape),
        in_specs=[
            SCALARS,
            HBM,
            pl.BlockSpec((27, block, height, length), lambda i: (0, i, 0, 0)),
        ],
        out_specs=WHOLE,
        compiler_params=params(16),
        cost_estimate=cost(27 * 12 * width * height * length, 8 * populations.size),
        name="collide_first",
    )(relax_rates, sent, populations)
    parity = lax.rem(lax.axis_index("span"), 2).astype(jnp.int32).reshape(1)
    own = near(30, width, length)
    field, up, down = pl.pallas_call(
        deposit_kernel,
        out_shape=[near(2, 3, width, height, length), own, own],
        in_specs=[WHOLE, WHOLE],
        out_specs=[WHOLE] * 3,
        compiler_params=params(24),
        name="deposit",
    )(held(received), held(collided))
    low = lax.ppermute(up, "leaf", [(l, (l + 1) % leaves) for l in range(leaves)])
    high = lax.ppermute(down, "leaf", [(l, (l - 1) % leaves) for l in range(leaves)])
    padded = near(27, PLANES, height, length)
    final = pltpu.HBM(populations.shape, F32)
    faces = [held(each) for each in (up, down, low, high)]
    work = 27 * 12 * width * height * length
    streamed = pl.pallas_call(
        stream_kernel,
        out_shape=padded,
        in_specs=[WHOLE] * 2,
        out_specs=WHOLE,
        compiler_params=params(16),
        cost_estimate=cost(work, 4 * populations.size),
        name="stream_own",
    )(held(collided), held(field))
    layer = near(45, height, length)
    a_sent, b_sent = pl.pallas_call(
        side_kernel,
        out_shape=[layer, layer],
        in_specs=[SCALARS, WHOLE, WHOLE, HBM, WHOLE, WHOLE],
        out_specs=[WHOLE] * 2,
        compiler_params=params(16),
        name="side_layers",
    )(parity, held(collided), held(field), streamed, held(low), held(high))
    a_got = lax.ppermute(a_sent, "span", [(s, s ^ 1) for s in range(spans)])
    b_got = lax.ppermute(
        b_sent, "span", [(s, (s + 1 if s % 2 else s - 1) % spans) for s in range(spans)]
    )
    state, result, ring = pl.pallas_call(
        inner_kernel,
        out_shape=[padded, padded, near(2, 9, 24, length)],
        in_specs=[SCALARS] + [WHOLE] * 6,
        out_specs=[WHOLE] * 3,
        input_output_aliases={1: 0},
        compiler_params=params(16),
        cost_estimate=cost(work, 4 * populations.size),
        name="first_planes",
    )(relax_rates, held(streamed), held(field), *faces)
    out, result = pl.pallas_call(
        more_kernel,
        out_shape=[final, padded],
        in_specs=[SCALARS] + [WHOLE] * 4,
        out_specs=[HBM, WHOLE],
        input_output_aliases={4: 1},
        scratch_shapes=[pltpu.SemaphoreType.DMA((width // 2,))],
        compiler_params=params(16),
        cost_estimate=cost(work, 4 * populations.size),
        name="more_planes",
    )(relax_rates, held(state), held(field), held(ring), held(result))
    corner = near(15, 8, length)
    halo, up_corner, down_corner, low_corner, high_corner = pl.pallas_call(
        corner_kernel,
        out_shape=[near(2, 45, height, length)] + [corner] * 4,
        in_specs=[SCALARS] + [WHOLE] * 2 + [HBM],
        out_specs=[WHOLE] * 5,
        compiler_params=params(16),
        name="corners",
    )(parity, held(a_got), held(b_got), result)
    corners = [held(each) for each in (up_corner, down_corner, low_corner, high_corner)]
    return pl.pallas_call(
        outer_kernel,
        out_shape=[final, padded, padded],
        in_specs=[SCALARS, WHOLE, WHOLE, WHOLE, HBM] + [WHOLE] * 9,
        out_specs=[HBM, WHOLE, WHOLE],
        input_output_aliases={2: 1, 3: 2, 4: 0},
        scratch_shapes=[
            pltpu.VMEM((2, 30, 8, length), F32),
            pltpu.VMEM((2, 9, 8, length), F32),
            pltpu.VMEM((2, 9, 8, length), F32),
            pltpu.SemaphoreType.DMA((3,)),
        ],
        compiler_params=params(16),
        name="outer_planes",
    )(relax_rates, held(halo), held(state), held(result), far(out), held(field), *faces, *corners)[0]


def solution(mesh):
    placed = (
        P(None, "span", "leaf", None),
        P(),
        P(None, None, ("span", "leaf")),
        P(None, ("span", "leaf"), None),
        P(None, ("span", "leaf")),
    )
    return jax.shard_map(
        body, mesh=mesh, in_specs=placed, out_specs=P(None, "span", "leaf", None), check_vma=False
    )
```

```python
import functools
import jax
import jax.numpy as jnp
import numpy as np
from jax import lax
from jax.experimental import pallas as pl
from jax.experimental.pallas import tpu as pltpu
from jax.sharding import PartitionSpec as P

F32 = jnp.float32
BF16 = jnp.bfloat16
SPLIT = 7
PLANES = 20
WHOLE = pl.BlockSpec(memory_space=pltpu.VMEM)
SCALARS = pl.BlockSpec(memory_space=pltpu.SMEM)
HBM = pl.BlockSpec(memory_space=pl.ANY)


def params(mib):
    return pltpu.CompilerParams(vmem_limit_bytes=mib * 2**20)


def components(q):
    return q // 9 - 1, (q // 3) % 3 - 1, q % 3 - 1


def transform(values, step):
    values = list(values)
    for stride in (9, 3, 1):
        for q in range(27):
            if (q // stride) % 3 == 0:
                triple = (q, q + stride, q + 2 * stride)
                for place, value in zip(triple, step(*[values[i] for i in triple])):
                    values[place] = value
    return values


def to_moments(low, middle, high):
    both = low + high
    return both + middle, high - low, both


def from_moments(zeroth, first, second):
    return second - first, zeroth - second, second + first


def collide(populations, rate, force):
    moments = transform(populations, to_moments)
    density = moments[0]
    momentum = (moments[9], moments[3], moments[1])
    velocity = [part * (1.0 / 27.0) for part in momentum]
    flux = [27.0 * part for part in velocity]
    energy = [3.0 * f * v for f, v in zip(flux, velocity)]
    cross = {}
    for i in range(3):
        for j in range(i + 1, 3):
            cross[i, j] = flux[i] * velocity[j]
    relaxed = []
    for k in range(27):
        powers = (k // 9, (k // 3) % 3, k % 3)
        odd = [i for i in range(3) if powers[i] == 1]
        squares = [i for i in range(3) if powers[i] == 2]
        share = 3.0 ** -len(squares)
        if len(odd) == 0:
            level = density
            for i in squares:
                level = level + energy[i]
        elif len(odd) == 1:
            level = flux[odd[0]]
        elif len(odd) == 2:
            level = cross[odd[0], odd[1]]
        else:
            level = None
        if level is not None and squares:
            level = level * share
        gap = moments[k] if level is None else moments[k] - level
        value = moments[k] - rate(k) * gap
        if force is not None and len(odd) == 1:
            push = force[odd[0]]
            value = value + (push * share if squares else push)
        relaxed.append(value)
    result = transform(relaxed, from_moments)
    scaled = []
    for q in range(27):
        moving = sum(1 for c in components(q) if c != 0)
        scaled.append(result[q] * 0.5**moving if moving else result[q])
    return scaled


def sources(force):
    weight = {1: 2.0 / 9.0, 2: 1.0 / 18.0, 3: 1.0 / 72.0}
    scaled = {n: [part * weight[n] for part in force] for n in weight}
    terms = [None] * 27
    for q in range(14, 27):
        c = components(q)
        total = None
        for i in range(3):
            if c[i] == 0:
                continue
            part = scaled[sum(1 for v in c if v != 0)][i]
            if total is None:
                total = part
            elif c[i] > 0:
                total = total + part
            else:
                total = total - part
        terms[q] = (total, 1)
        terms[26 - q] = (total, -1)
    return terms


def pushed(value, term):
    if term is None:
        return value
    return value + term[0] if term[1] > 0 else value - term[0]


def group_order(leaves):
    root = leaves * 5 // 8
    return [root] + [leaf for leaf in range(leaves) if leaf != root]


def bin_kernel(forces_hbm, dest_hbm, cells_hbm, sent_ref, forces_ref, dest_ref, cells_ref, sems):
    pairs = ((dest_hbm, dest_ref), (cells_hbm, cells_ref), (forces_hbm, forces_ref))
    copies = [pltpu.make_async_copy(a, b, sems.at[i]) for i, (a, b) in enumerate(pairs)]
    for each in copies:
        each.start()
    markers = cells_ref.shape[1]
    leaves = sent_ref.shape[0]
    root = leaves * 5 // 8
    earlier = (
        lax.broadcasted_iota(jnp.int32, (markers, markers), 0)
        < lax.broadcasted_iota(jnp.int32, (markers, markers), 1)
    ).astype(F32).astype(BF16)
    copies[0].wait()
    hot = []
    for t in range(2):
        row = dest_ref[t]
        row = jnp.where(row < root, row + 1, jnp.where(row == root, 0, row))
        leaf = lax.broadcasted_iota(jnp.int32, (leaves, markers), 0)
        hot.append((leaf == row).astype(F32))
    ahead = jnp.dot(
        jnp.concatenate(hot, axis=0).astype(BF16), earlier, preferred_element_type=F32
    )
    copies[1].wait()
    copies[2].wait()
    left, right = [], []
    for t in range(2):
        rank = jnp.sum(hot[t] * ahead[t * leaves : (t + 1) * leaves], axis=0, keepdims=True)
        rank = rank.astype(jnp.int32)
        third = rank // 16
        left.append(jnp.concatenate([jnp.where(third == r, hot[t], 0.0) for r in range(3)], axis=0))
        spot = lax.broadcasted_iota(jnp.int32, (16, markers), 0) == rank % 16
        rows = [cells_ref[t : t + 1, :].astype(F32)] + [forces_ref[c, t : t + 1, :] for c in range(3)]
        own = jnp.concatenate([jnp.where(spot, row, 0.0) for row in rows], axis=0)
        none = jnp.zeros_like(own)
        right.append(jnp.concatenate([own, none] if t == 0 else [none, own], axis=0))
    values = jnp.concatenate(right, axis=1)
    parts = []
    for _ in range(3):
        part = values.astype(BF16)
        parts.append(part)
        values = values - part.astype(F32)
    packed = lax.dot_general(
        jnp.concatenate(left, axis=1).astype(BF16),
        jnp.concatenate(parts, axis=0),
        (((1,), (1,)), ((), ())),
        preferred_element_type=F32,
    )
    packed = packed[:, :128] + packed[:, 128:256] + packed[:, 256:]
    for r in range(3):
        sent_ref[:, 0, 128 * r : 128 * r + 128] = packed[r * leaves : (r + 1) * leaves]


def first_kernel(rates_ref, after_ref, populations_ref, collided_ref):
    width = populations_ref.shape[1]
    base = pl.program_id(0) * width

    def plane(x, carry):
        result = collide(
            [populations_ref[q, x] for q in range(27)], lambda k: rates_ref[k], None
        )
        for q in range(27):
            collided_ref[q, base + x] = result[q]
        return carry

    lax.fori_loop(0, width, plane, 0, unroll=2)


def rows_by_value(received_ref):
    blocks = []
    for r in range(2):
        whole = received_ref[:, 0, 128 * r : 128 * r + 128]
        blocks += [whole[8 * b : 8 * b + 8] for b in range(4)]
    lane = lax.broadcasted_iota(jnp.int32, (8, 128), 1)
    for half in (4, 2, 1):
        low = (lane // (16 * half)) % 2 == 0
        for b in range(8):
            if b & half:
                continue
            first, second = blocks[b], blocks[b + half]
            blocks[b] = jnp.where(low, first, pltpu.roll(second, 16 * half, 1))
            blocks[b + half] = jnp.where(low, pltpu.roll(first, 128 - 16 * half, 1), second)
    last = received_ref[:, 0, 256:384]
    tail = None
    for b in range(4):
        part = last[8 * b : 8 * b + 8]
        part = jnp.where(lane % 16 < 4, part, 0.0)
        if b:
            part = pltpu.roll(part, 4 * b, 1)
        tail = part if tail is None else tail + part
    sub = lax.broadcasted_iota(jnp.int32, (8, 128), 0)
    rows = []
    for v in range(8):
        spread = pltpu.roll(tail, 128 - 16 * v, 1) if v else tail
        spread = pltpu.roll(spread, 0, 1, stride=16, stride_axis=0)
        spread = jnp.where(lane // 16 == sub, spread, 0.0)
        rows.append((blocks[v], jnp.sum(spread, axis=0, keepdims=True)))
    return rows


def rows_of(height, sign):
    edge, inside = (height - 1, height - 2) if sign > 0 else (0, 1)
    return ((edge, 0, (0, sign)), (inside, 18, (sign,)))


def own_faces(collided_ref, field_ref, up_ref, down_ref):
    height = collided_ref.shape[2]
    for ref, sign in ((up_ref, 1), (down_ref, -1)):
        for z, first, kinds in rows_of(height, sign):
            terms = sources([field_ref[0, c, :, z, :] for c in range(3)])
            for order, cz in enumerate(kinds):
                for j in range(9):
                    q = 3 * j + cz + 1
                    ref[first + 9 * order + j] = pushed(collided_ref[q, :, z, :], terms[q])
        for c in range(3):
            ref[27 + c] = field_ref[1, c, :, height - 1 if sign > 0 else 0, :]


def deposit_kernel(received_ref, collided_ref, field_ref, up_ref, down_ref):
    rows = rows_by_value(received_ref)
    index = lax.broadcasted_iota(jnp.int32, (128, 128), 0).astype(F32).astype(BF16)
    one, zero = jnp.ones((), BF16), jnp.zeros((), BF16)
    for t in range(2):
        values = rows[4 * t : 4 * t + 4]
        chunks = [[v[0][s : s + 1] for s in range(8)] + [v[1]] for v in values]
        outer, weighted = [], []
        for s in range(9):
            cell = chunks[0][s].astype(jnp.int32)
            outer.append(jnp.where(index == (cell // 128).astype(F32).astype(BF16), one, zero))
            inner = index == (cell % 128).astype(F32).astype(BF16)
            parts = []
            for c in range(3):
                amount = chunks[c + 1][s]
                big = amount.astype(BF16)
                small = (amount - big.astype(F32)).astype(BF16)
                parts.append((jnp.where(inner, big, zero), jnp.where(inner, small, zero)))
            weighted.append(
                jnp.concatenate([p[0] for p in parts] + [p[1] for p in parts], axis=0)
            )
        field = lax.dot_general(
            jnp.concatenate(weighted, axis=1),
            jnp.concatenate(outer, axis=1),
            (((1,), (1,)), ((), ())),
            preferred_element_type=F32,
        )
        for c in range(3):
            whole = field[128 * c : 128 * c + 128] + field[384 + 128 * c : 512 + 128 * c]
            field_ref[t, c] = whole.T.reshape(field_ref.shape[2:])
    own_faces(collided_ref, field_ref, up_ref, down_ref)


def corner_at(place, number):
    return place // 2, pl.ds(4 * (place % 2) + number, 1)


def layer_row(n, number, cz):
    return 30 + n // 4, pl.ds(2 * (n % 4) + number - (1 - cz if cz >= 0 else 2), 1)


def side_kernel(parity_ref, collided_ref, field_ref, after_ref, low_ref, high_ref, a_ref, b_ref):
    last = collided_ref.shape[1] - 1

    def layers(ref, sign, edge, inside):
        def put(n, number, cz, got, place, x):
            tile, row = layer_row(n, number, cz)
            ref[tile, row, :] = got[place, pl.ds(x, 1), :]

        for first, count, x in ((0, 18, edge), (18, 9, inside)):
            terms = sources([field_ref[0, c, x] for c in range(3)])
            for n in range(first, first + count):
                q = 9 + n if n < 9 else 9 + 9 * sign + n % 9
                j, cz = q // 3, q % 3 - 1
                ref[n] = pushed(collided_ref[q, x], terms[q])
                if cz >= 0:
                    put(n, 1, cz, low_ref, 9 * cz + j, x)
                if cz <= 0:
                    put(n, 2, cz, high_ref, -9 * cz + j, x)
                if cz > 0:
                    put(n, 0, cz, low_ref, 18 + j, x)
                if cz < 0:
                    put(n, 3, cz, high_ref, 18 + j, x)
        for c in range(3):
            ref[27 + c] = field_ref[1, c, edge]
            put(27 + c, 1, 0, low_ref, 27 + c, edge)
            put(27 + c, 2, 0, high_ref, 27 + c, edge)

    @pl.when(parity_ref[0] == 0)
    def _():
        layers(a_ref, 1, last, last - 1)
        layers(b_ref, -1, 0, 1)

    @pl.when(parity_ref[0] != 0)
    def _():
        layers(b_ref, 1, last, last - 1)
        layers(a_ref, -1, 0, 1)


def corner_kernel(
    parity_ref, a_ref, b_ref, after_ref,
    halo_ref, up_ref, down_ref, low_ref, high_ref,
):
    @pl.when(parity_ref[0] == 0)
    def _():
        halo_ref[0] = b_ref[...]
        halo_ref[1] = a_ref[...]

    @pl.when(parity_ref[0] != 0)
    def _():
        halo_ref[0] = a_ref[...]
        halo_ref[1] = b_ref[...]

    height = a_ref.shape[1]

    def columns(place, cz, load, ref):
        cx = (place % 9) // 3 - 1
        n = 3 * (place % 3) + cz + 1
        for side, toward, near, far in ((0, 1, 1, 0), (1, -1, 2, 3)):
            wanted = [(near, n)] if cx == 0 else []
            if cx == toward:
                wanted = [(near, 9 + n), (far, 18 + n)]
            for number, layer in wanted:
                tile, row = corner_at(place, number)
                ref[tile, row, :] = load(side, layer)

    def outside(number, cz):
        def load(side, layer):
            tile, row = layer_row(layer, number, cz)
            return halo_ref[side, tile, row, :]

        return load

    for ref, own_ref, sign, first, z in (
        (low_ref, down_ref, 1, 1, 0),
        (high_ref, up_ref, -1, 2, height - 1),
    ):
        for j in range(9):
            columns(j, 0, outside(first, 0), ref)
            columns(9 + j, sign, outside(first, sign), ref)
            columns(18 + j, sign, outside(first - sign, sign), ref)
            columns(9 + j, -sign, lambda side, n: halo_ref[side, n, pl.ds(z, 1), :], own_ref)
        for c in range(3):
            for side, number in ((0, 1), (1, 2)):
                tile, row = corner_at(27 + c, number)
                ref[tile, row, :] = outside(first, 0)(side, 27 + c)


def moved(tile, q, low_row, high_row):
    _, cy, cz = components(q)
    height = tile.shape[0]
    if cz:
        sub = lax.broadcasted_iota(jnp.int32, tile.shape, 0)
        if cz > 0:
            tile = jnp.where(sub == 0, low_row(), pltpu.roll(tile, 1, 0))
        else:
            tile = jnp.where(sub == height - 1, high_row(), pltpu.roll(tile, height - 1, 0))
    return pltpu.roll(tile, cy % 128, 1) if cy else tile


def edge_rows(got, sent, toward, start, force, rate):
    values = []
    for q in range(27):
        cx, cy, cz = components(q)
        j = q // 3
        where = pl.ds(start - cx, 8)
        if cz == toward:
            row = got(18 + j, where)
        elif cz == 0:
            row = got(j, where)
        else:
            row = sent(9 + j, where)
        values.append(pltpu.roll(row, cy % 128, 1) if cy else row)
    after = collide(values, rate, force)
    return [after[3 * j + toward + 1] for j in range(9)]


def second(x, force, rate, state, ring, result, row=None):
    row = x if row is None else row
    after = collide([state[q, x] for q in range(27)], rate, force)
    for q in range(27):
        j = q // 3
        result[q, x + q // 9 - 1] = moved(
            after[q],
            q,
            lambda: ring[0, j, pl.ds(row, 1), :],
            lambda: ring[1, j, pl.ds(row, 1), :],
        )


def write_out(result, out_ref, sem, plane, count):
    return pltpu.make_async_copy(
        result.at[:, pl.ds(2 + plane, count)], out_ref.at[:, pl.ds(plane, count)], sem
    )


def planes(first, last, rate, field_ref, state, ring, result):
    def plane(x, carry):
        second(x + 2, [field_ref[1, c, x] for c in range(3)], rate, state, ring, result)
        return carry

    lax.fori_loop(first, last, plane, 0, unroll=2)


def stream_kernel(collided_ref, field_ref, state):
    def own(x, carry):
        terms = sources([field_ref[0, c, x] for c in range(3)])
        for q in range(27):
            cx, cy, cz = components(q)
            tile = pushed(collided_ref[q, x], terms[q])
            if cz:
                tile = pltpu.roll(tile, cz % tile.shape[0], 0)
            if cy:
                tile = pltpu.roll(tile, cy % 128, 1)
            state[q, x + 2 + cx] = tile
        return carry

    lax.fori_loop(0, collided_ref.shape[1], own, 0, unroll=2)


def inner_kernel(
    rates_ref, state_in, field_ref, up_ref, down_ref, low_ref, high_ref,
    state, result, ring,
):
    width, height = field_ref.shape[2:4]
    rate = lambda k: rates_ref[k]
    for q in range(27):
        cx, cy, cz = components(q)
        if cz == 0:
            continue
        got, z = (low_ref, 0) if cz > 0 else (high_ref, height - 1)
        rows = got[9 + q // 3]
        state[q, pl.ds(2 + cx, width), z, :] = pltpu.roll(rows, cy % 128, 1) if cy else rows
    for side, got, sent, toward in ((0, low_ref, down_ref, 1), (1, high_ref, up_ref, -1)):

        def edge(block, carry, side=side, got=got, sent=sent, toward=toward):
            start = 1 + (width - 10) * block
            force = [got[27 + c, pl.ds(start, 8), :] for c in range(3)]
            rows = edge_rows(
                lambda place, where: got[place, where, :],
                lambda place, where: sent[place, where, :],
                toward, start, force, rate,
            )
            for j in range(9):
                ring[side, j, pl.ds(start + 2, 8), :] = rows[j]
            return carry

        lax.fori_loop(0, 2, edge, 0, unroll=2)
    planes(1, SPLIT, rate, field_ref, state, ring, result)


def more_kernel(rates_ref, state, field_ref, ring, result_in, out_ref, result, sems):
    width = field_ref.shape[2]
    rate = lambda k: rates_ref[k]
    copies = [write_out(result, out_ref, sems.at[0], 2, SPLIT - 3)]
    copies[0].start()
    done = SPLIT
    for place in range(SPLIT - 1, width - 4, 2):
        planes(done, place + 3, rate, field_ref, state, ring, result)
        done = place + 3
        copies.append(write_out(result, out_ref, sems.at[len(copies)], place, 2))
        copies[-1].start()
    planes(done, width - 1, rate, field_ref, state, ring, result)
    for each in copies:
        each.wait()


def outer_kernel(
    rates_ref, halo_ref, state_in, result_in, out_in, field_ref,
    up_ref, down_ref, low_ref, high_ref,
    up_corner, down_corner, low_corner, high_corner,
    out_ref, state, result, got, sent, ring, sems,
):
    width = field_ref.shape[2]
    rate = lambda k: rates_ref[k]
    ready = write_out(result, out_ref, sems.at[2], width - 4, 2)
    ready.start()
    columns = (0, 1, width + 2, width + 3)
    for side, toward, near in ((0, 1, 1), (1, -1, width + 2)):
        for n in range(27):
            q = 9 + n if n < 9 else 9 + 9 * toward + n % 9
            column = near if n < 18 else near - toward
            place = 9 + q // 3
            tile, row = corner_at(place, columns.index(column))
            state[q, column + q // 9 - 1] = moved(
                halo_ref[side, n],
                q,
                lambda: low_corner[tile, row, :],
                lambda: high_corner[tile, row, :],
            )

    def gather(target, place, own, corner, source):
        tile, row = source // 2, 4 * (source % 2)
        target[place, pl.ds(0, 2), :] = corner[tile, pl.ds(row, 2), :]
        target[place, pl.ds(2, 2), :] = own[source, pl.ds(0, 2), :]
        target[place, pl.ds(4, 2), :] = own[source, pl.ds(width - 2, 2), :]
        target[place, pl.ds(6, 2), :] = corner[tile, pl.ds(row + 2, 2), :]

    sides = (
        (0, low_ref, low_corner, down_ref, down_corner, 1),
        (1, high_ref, high_corner, up_ref, up_corner, -1),
    )
    for side, mine, corner, left, left_corner, toward in sides:
        for place in list(range(9)) + list(range(18, 30)):
            gather(got.at[side], place, mine, corner, place)
        for j in range(9):
            gather(sent.at[side], j, left, left_corner, 9 + j)
        values = []
        for q in range(27):
            cx, cy, cz = components(q)
            j = q // 3
            if cz == toward:
                row = got[side, 18 + j]
            elif cz == 0:
                row = got[side, j]
            else:
                row = sent[side, j]
            if cx:
                row = pltpu.roll(row, cx % 8, 0)
            values.append(pltpu.roll(row, cy % 128, 1) if cy else row)
        after = collide(values, rate, [got[side, 27 + c] for c in range(3)])
        for j in range(9):
            ring[side, j] = after[3 * j + toward + 1]

    def plane(x, row, force):
        second(x, force, rate, state, ring, result, row)

    plane(1, 1, [halo_ref[0, 27 + c] for c in range(3)])
    plane(2, 2, [field_ref[1, c, 0] for c in range(3)])
    first = write_out(result, out_ref, sems.at[0], 0, 2)
    first.start()
    plane(width + 1, 5, [field_ref[1, c, width - 1] for c in range(3)])
    plane(width + 2, 6, [halo_ref[1, 27 + c] for c in range(3)])
    last = write_out(result, out_ref, sems.at[1], width - 2, 2)
    last.start()
    ready.wait()
    first.wait()
    last.wait()


def cost(flops, moved):
    return pl.CostEstimate(flops=flops, bytes_accessed=moved, transcendentals=0)


def body(populations, relax_rates, marker_forces, marker_dest, marker_cells):
    width, height, length = populations.shape[1:]
    leaves = lax.axis_size("leaf")
    spans = lax.axis_size("span")
    markers = marker_cells.shape[1]
    held = functools.partial(pltpu.with_memory_space_constraint, memory_space=pltpu.VMEM)
    far = functools.partial(pltpu.with_memory_space_constraint, memory_space=pltpu.HBM)
    near = lambda *shape: pltpu.VMEM(shape, F32)
    sent = pl.pallas_call(
        bin_kernel,
        out_shape=near(leaves, 1, 384),
        in_specs=[HBM] * 3,
        out_specs=WHOLE,
        scratch_shapes=[
            pltpu.VMEM((3, 2, markers), F32),
            pltpu.VMEM((2, 1, markers), jnp.int32),
            pltpu.VMEM((2, markers), jnp.int32),
            pltpu.SemaphoreType.DMA((3,)),
        ],
        compiler_params=params(16),
        name="bin_markers",
    )(
        far(jnp.transpose(marker_forces, (1, 0, 2))),
        far(jnp.transpose(marker_dest, (0, 2, 1))),
        far(marker_cells),
    )
    received = lax.all_to_all(
        sent, "leaf", 0, 0, tiled=True, axis_index_groups=[group_order(leaves)]
    )
    block = 2
    collided = pl.pallas_call(
        first_kernel,
        grid=(width // block,),
        out_shape=near(*populations.shape),
        in_specs=[
            SCALARS,
            HBM,
            pl.BlockSpec((27, block, height, length), lambda i: (0, i, 0, 0)),
        ],
        out_specs=WHOLE,
        compiler_params=params(16),
        cost_estimate=cost(27 * 12 * width * height * length, 8 * populations.size),
        name="collide_first",
    )(relax_rates, sent, populations)
    parity = lax.rem(lax.axis_index("span"), 2).astype(jnp.int32).reshape(1)
    own = near(30, width, length)
    field, up, down = pl.pallas_call(
        deposit_kernel,
        out_shape=[near(2, 3, width, height, length), own, own],
        in_specs=[WHOLE, WHOLE],
        out_specs=[WHOLE] * 3,
        compiler_params=params(24),
        name="deposit",
    )(held(received), held(collided))
    low = lax.ppermute(up, "leaf", [(l, (l + 1) % leaves) for l in range(leaves)])
    high = lax.ppermute(down, "leaf", [(l, (l - 1) % leaves) for l in range(leaves)])
    padded = near(27, PLANES, height, length)
    final = pltpu.HBM(populations.shape, F32)
    faces = [held(each) for each in (up, down, low, high)]
    work = 27 * 12 * width * height * length
    streamed = pl.pallas_call(
        stream_kernel,
        out_shape=padded,
        in_specs=[WHOLE] * 2,
        out_specs=WHOLE,
        compiler_params=params(16),
        cost_estimate=cost(work, 4 * populations.size),
        name="stream_own",
    )(held(collided), held(field))
    layer = near(38, height, length)
    a_sent, b_sent = pl.pallas_call(
        side_kernel,
        out_shape=[layer, layer],
        in_specs=[SCALARS, WHOLE, WHOLE, HBM, WHOLE, WHOLE],
        out_specs=[WHOLE] * 2,
        compiler_params=params(16),
        name="side_layers",
    )(parity, held(collided), held(field), streamed, held(low), held(high))
    a_got = lax.ppermute(a_sent, "span", [(s, s ^ 1) for s in range(spans)])
    b_got = lax.ppermute(
        b_sent, "span", [(s, (s + 1 if s % 2 else s - 1) % spans) for s in range(spans)]
    )
    state, result, ring = pl.pallas_call(
        inner_kernel,
        out_shape=[padded, padded, near(2, 9, 24, length)],
        in_specs=[SCALARS] + [WHOLE] * 6,
        out_specs=[WHOLE] * 3,
        input_output_aliases={1: 0},
        compiler_params=params(16),
        cost_estimate=cost(work, 4 * populations.size),
        name="first_planes",
    )(relax_rates, held(streamed), held(field), *faces)
    out, result = pl.pallas_call(
        more_kernel,
        out_shape=[final, padded],
        in_specs=[SCALARS] + [WHOLE] * 4,
        out_specs=[HBM, WHOLE],
        input_output_aliases={4: 1},
        scratch_shapes=[pltpu.SemaphoreType.DMA((width // 2,))],
        compiler_params=params(16),
        cost_estimate=cost(work, 4 * populations.size),
        name="more_planes",
    )(relax_rates, held(state), held(field), held(ring), held(result))
    corner = near(15, 8, length)
    halo, up_corner, down_corner, low_corner, high_corner = pl.pallas_call(
        corner_kernel,
        out_shape=[near(2, 38, height, length)] + [corner] * 4,
        in_specs=[SCALARS] + [WHOLE] * 2 + [HBM],
        out_specs=[WHOLE] * 5,
        compiler_params=params(16),
        name="corners",
    )(parity, held(a_got), held(b_got), result)
    corners = [held(each) for each in (up_corner, down_corner, low_corner, high_corner)]
    return pl.pallas_call(
        outer_kernel,
        out_shape=[final, padded, padded],
        in_specs=[SCALARS, WHOLE, WHOLE, WHOLE, HBM] + [WHOLE] * 9,
        out_specs=[HBM, WHOLE, WHOLE],
        input_output_aliases={2: 1, 3: 2, 4: 0},
        scratch_shapes=[
            pltpu.VMEM((2, 30, 8, length), F32),
            pltpu.VMEM((2, 9, 8, length), F32),
            pltpu.VMEM((2, 9, 8, length), F32),
            pltpu.SemaphoreType.DMA((3,)),
        ],
        compiler_params=params(16),
        name="outer_planes",
    )(relax_rates, held(halo), held(state), held(result), far(out), held(field), *faces, *corners)[0]


def solution(mesh):
    placed = (
        P(None, "span", "leaf", None),
        P(),
        P(None, None, ("span", "leaf")),
        P(None, ("span", "leaf"), None),
        P(None, ("span", "leaf")),
    )
    return jax.shard_map(
        body, mesh=mesh, in_specs=placed, out_specs=P(None, "span", "leaf", None), check_vma=False
    )
```
